32 devices in a mesh: layer: 4 (over z), col: 8 (over y, x, core).
Axes of the slice: x: 2, y: 2, z: 4, core: 2. Of those that a mesh axis runs over, the one named last changes fastest.
Arguments:
- factors: bfloat16 [4, 8, 2048, 64], P('layer', 'col'), may hold values from -0.9 to 0.9
- cores: float32 [4, 64, 64], P('layer'), may hold values from -2 to 6, as said below
- tile_list: int32 [64, 2], P('col'), may hold values from 0 to 7, as said below
- probes: bfloat16 [2048, 64, 64], P(None, 'col'), may hold values from -6 to 6
Outputs:
- basis: float32 [2048, 64, 64], P('layer', 'col')
- update_right: float32 [2048, 64, 64], P('layer', 'col')
The draws below stay inside these ranges and needn't reach their ends.
Inputs may be any that keep to these rules, and one draw needn't show every extreme that they name: `tile_list`: each row is a block row and a block column of a tile of the lower triangle: the first is not below the second. `cores`: each matrix is symmetric positive definite: a Gram matrix plus a positive diagonal.
All inputs are finite; a program needn't handle non-finite values.
Results may differ from the reference program's by a relative error of at most 0.02.
Values may be sent and summed in bfloat16 or wider, within the bound.
A program may use at most 64 MiB of HBM per device.

```python
import math
import jax
import jax.numpy as jnp
from jax import lax

B = 2048
R = 64
PAN_DEV = 1
PANELS = 4
ROWS = 8
NT = 64
N_LAYER = 4


def draw_factors(key, part):
    key_main = jax.random.fold_in(key, 31)
    shape = (PANELS, ROWS, B, R)
    values = jnp.clip(0.15 * jax.random.normal(key_main, shape, jnp.float32), -0.9, 0.9)
    return values.astype(jnp.bfloat16)


def draw_probes(key, part):
    key_main = jax.random.fold_in(key, 41)
    shape = (B, NT, R)
    values = jnp.clip(jax.random.normal(key_main, shape, jnp.float32), -6.0, 6.0)
    return values.astype(jnp.bfloat16)


def draw_cores(key, part):
    key_base = jax.random.fold_in(key, 11)
    key_diag = jax.random.fold_in(key, 12)
    base = jax.random.normal(key_base, (PANELS, R, R), jnp.float32)
    spread = jax.random.uniform(key_diag, (PANELS, R), jnp.float32, 0.5, 2.0)
    gram = jnp.einsum('kab,kcb->kac', base, base) / R
    return gram + spread[:, :, None] * jnp.eye(R, dtype=jnp.float32)[None]


def draw_tile_list(key, part):
    key_one = jax.random.fold_in(key, 21)
    key_two = jax.random.fold_in(key, 22)
    first = jax.random.randint(key_one, (NT,), 0, ROWS)
    second = jax.random.randint(key_two, (NT,), 0, ROWS)
    upper = jnp.maximum(first, second)
    lower = jnp.minimum(first, second)
    upper = upper.at[0].set(ROWS - 1)
    lower = lower.at[0].set(0)
    return jnp.stack([upper, lower], axis=1).astype(jnp.int32)


def setup_inputs(seed: int = 0) -> dict:
    key_of = jax.random.split(jax.random.key(seed), 5)
    return {
        "factors": draw_factors(jax.random.fold_in(key_of[4], 71), 0),
        "cores": draw_cores(jax.random.fold_in(key_of[4], 71), 0),
        "tile_list": draw_tile_list(jax.random.fold_in(key_of[4], 71), 0),
        "probes": draw_probes(jax.random.fold_in(key_of[4], 71), 0),
    }


def reference(factors, cores, tile_list, probes):
    row_first = tile_list[:, 0].astype(jnp.int32)
    row_second = tile_list[:, 1].astype(jnp.int32)
    probe_full = probes.astype(jnp.float32)
    highest = lax.Precision.HIGHEST
    samples = jnp.zeros((B, NT, R), jnp.float32)
    for layer_group in range(N_LAYER):
        block = factors[layer_group * PAN_DEV:(layer_group + 1) * PAN_DEV]
        core_group = cores[layer_group * PAN_DEV:(layer_group + 1) * PAN_DEV]
        left_rows = jnp.take(block, row_first, axis=1).astype(jnp.float32)
        right_rows = jnp.take(block, row_second, axis=1).astype(jnp.float32)
        sketch = jnp.einsum('ktbr,bts->ktrs', right_rows, probe_full)
        core_first = jnp.einsum('kar,ktrs->ktas', core_group, sketch, precision=highest).astype(jnp.bfloat16)
        core_first = lax.optimization_barrier(core_first).astype(jnp.float32)
        part_sample = jnp.einsum('ktbr,ktrs->bts', left_rows, core_first).astype(jnp.bfloat16)
        samples = samples + lax.optimization_barrier(part_sample).astype(jnp.float32)
    gram = jnp.einsum('btr,bts->trs', samples, samples, precision=highest)
    chol = jnp.linalg.cholesky(gram)
    unit_matrix = jnp.broadcast_to(jnp.eye(R, dtype=jnp.float32), chol.shape)
    chol_inverse = jax.scipy.linalg.solve_triangular(chol, unit_matrix, lower=True)
    ortho = jnp.einsum('btr,tsr->bts', samples, chol_inverse, precision=highest)
    ortho_half = ortho.astype(jnp.bfloat16)
    ortho_half = lax.optimization_barrier(ortho_half).astype(jnp.float32)
    update_right = jnp.zeros((B, NT, R), jnp.float32)
    for layer_group in range(N_LAYER):
        block = factors[layer_group * PAN_DEV:(layer_group + 1) * PAN_DEV]
        core_group = cores[layer_group * PAN_DEV:(layer_group + 1) * PAN_DEV]
        left_rows = jnp.take(block, row_first, axis=1).astype(jnp.float32)
        right_rows = jnp.take(block, row_second, axis=1).astype(jnp.float32)
        projected = jnp.einsum('ktbr,bts->ktrs', left_rows, ortho_half)
        core_second = jnp.einsum('kar,ktrs->ktas', core_group, projected, precision=highest).astype(jnp.bfloat16)
        core_second = lax.optimization_barrier(core_second).astype(jnp.float32)
        part_right = jnp.einsum('ktbr,ktrs->bts', right_rows, core_second).astype(jnp.bfloat16)
        update_right = update_right + lax.optimization_barrier(part_right).astype(jnp.float32)
    basis = ortho * math.sqrt(B)
    return (basis, update_right)
```

```python
import functools
import math

import jax
import jax.numpy as jnp
from jax import lax
from jax.experimental import pallas as pl
from jax.experimental.pallas import tpu as pltpu
from jax.sharding import PartitionSpec as P

MESH = pl.DeviceIdType.MESH
HIGHEST = lax.Precision.HIGHEST
NN = (((1,), (0,)), ((), ()))
NT = (((1,), (1,)), ((), ()))


def dot(a, b, dims, precision=None):
    return lax.dot_general(a, b, dims, precision=precision, preferred_element_type=jnp.float32)


def invert_factor(gram, rank, count):
    shape = gram.shape
    row = lax.broadcasted_iota(jnp.int32, shape, 0)
    lane = lax.broadcasted_iota(jnp.int32, shape, 1)
    inside = lane % rank
    block = lane // rank
    inverse = jnp.where(row == inside, 1.0, 0.0).astype(jnp.float32)
    pivots = jnp.ones(shape, jnp.float32)
    rest = gram
    for j in range(rank):
        column = jnp.broadcast_to(rest[:, j : j + 1], shape)
        for q in range(1, count):
            at = q * rank + j
            column = jnp.where(block == q, jnp.broadcast_to(rest[:, at : at + 1], shape), column)
        pivot = column[j : j + 1, :]
        pivots = jnp.where(row == j, pivot, pivots)
        if j < rank - 1:
            scale = jnp.where(row > j, column * (1.0 / pivot), 0.0)
            inverse = inverse - scale * inverse[j : j + 1, :]
            rest = rest - scale * rest[j : j + 1, :]
    root = lax.rsqrt(pivots)
    root = root * (1.5 - 0.5 * pivots * root * root)
    return inverse * root


def kernel(nl, nc, tiles_ref, factor_ref, core_ref, probe_ref, basis_ref, right_ref,
           panel, shared, probe, cores, first, sample, gram_out, gram_in, proj_out, proj_in,
           inv, second, sem_local, s_core, r_core, s_panel, r_panel, f_panel, s_rows, r_rows,
           s_shared, f_shared, r_shared, s_first, r_first, s_gram, r_gram, s_proj, r_proj,
           s_inv, r_inv, s_second, r_second):
    l, c = lax.axis_index("layer"), lax.axis_index("col")
    rank, order = factor_ref.shape
    nt = probe_ref.shape[0]
    share = order // nl
    per = -(-nt // nl)
    owners = nt // per
    half = 2 if nc % 2 == 0 else 1
    peers = nc // half
    group, side = c // half, c % half
    other = group * half + (half - 1 - side)

    def at_layer(k):
        return (k, c)

    def at_col(d):
        return (l, d)

    def peer(off):
        return lax.rem(group + off, peers) * half + side

    def next_layer(off):
        return lax.rem(l + off, nl)

    def remote(src, dst, send, recv, device):
        return pltpu.make_async_remote_copy(
            src_ref=src, dst_ref=dst, send_sem=send, recv_sem=recv, device_id=device,
            device_id_type=MESH)

    def when(everyone, pred, body):
        if everyone:
            body()
        else:
            pl.when(pred)(body)

    all_own = owners == nl

    def columns(k):
        return pl.ds(pl.multiple_of(k * share, share), share)

    barrier = pltpu.get_barrier_semaphore()
    for off in range(1, nl):
        pl.semaphore_signal(barrier, inc=1, device_id=at_layer(next_layer(off)), device_id_type=MESH)
    for off in range(1, peers):
        pl.semaphore_signal(barrier, inc=1, device_id=at_col(peer(off)), device_id_type=MESH)
    if half == 2:
        pl.semaphore_signal(barrier, inc=1, device_id=at_col(other), device_id_type=MESH)
    pl.semaphore_wait(barrier, nl - 1 + peers - 1 + half - 1)

    def core_copy(off):
        k = next_layer(off)
        return remote(core_ref, cores.at[l], s_core.at[k], r_core.at[l], at_layer(k))

    def core_arrival(k):
        return remote(core_ref, cores.at[k], s_core.at[k], r_core.at[k], at_layer(k))

    def rows_copy(off):
        k = next_layer(off)
        return remote(factor_ref.at[:, columns(k)], shared.at[c, l], s_rows.at[k], r_rows.at[l],
                      at_layer(k))

    def rows_arrival(k):
        return remote(shared.at[c, k], shared.at[c, k], s_rows.at[k], r_rows.at[k], at_layer(k))

    def panel_copy(off):
        return remote(factor_ref, panel.at[c], s_panel.at[off], r_panel.at[c], at_col(peer(off)))

    def panel_forward(off):
        d = peer(off)
        src = factor_ref if off == 0 else panel.at[d]
        return remote(src, panel.at[d], f_panel.at[off], r_panel.at[d], at_col(other))

    def panel_arrival(d):
        return remote(panel.at[d], panel.at[d], f_panel.at[0], r_panel.at[d], at_col(d))

    def shared_copy(off, k):
        return remote(shared.at[c, k], shared.at[c, k], s_shared.at[off, k], r_shared.at[c, k],
                      at_col(peer(off)))

    def shared_forward(off, k):
        d = peer(off)
        return remote(shared.at[d, k], shared.at[d, k], f_shared.at[off, k], r_shared.at[d, k],
                      at_col(other))

    def shared_arrival(d, k):
        return remote(shared.at[d, k], shared.at[d, k], f_shared.at[0, k], r_shared.at[d, k],
                      at_col(d))

    def exchange(buf_from, buf_to, send, recv, off):
        k = next_layer(off)
        return remote(buf_from(k), buf_to(l), send.at[k], recv.at[l], at_layer(k))

    def arrival(buf_to, send, recv, k):
        return remote(buf_to(k), buf_to(k), send.at[k], recv.at[k], at_layer(k))

    for off in range(1, nl):
        rows_copy(off).start()
    for off in range(1, peers):
        panel_copy(off).start()
    if half == 2:
        panel_forward(0).start()
    for off in range(1, nl):
        core_copy(off).start()
    copies = [
        pltpu.make_async_copy(probe_ref, probe, sem_local.at[0]),
        pltpu.make_async_copy(factor_ref, panel.at[c], sem_local.at[1]),
        pltpu.make_async_copy(factor_ref.at[:, columns(l)], shared.at[c, l], sem_local.at[2]),
        pltpu.make_async_copy(core_ref, cores.at[l], sem_local.at[3]),
    ]
    for copy in copies:
        copy.start()

    for off in range(1, peers):
        panel_arrival(peer(off)).wait_recv()
        if half == 2:
            panel_forward(off).start()

    def send_shared(off, carry):
        k = next_layer(off)
        rows_arrival(k).wait_recv()
        for hop in range(1, peers):
            shared_copy(hop, k).start()
        if half == 2:
            shared_forward(0, k).start()
        return carry

    lax.fori_loop(1, nl, send_shared, 0)
    for copy in copies:
        copy.wait()
    if half == 2:
        for off in range(peers):
            panel_arrival(lax.rem(group + off, peers) * half + (1 - side)).wait_recv()

    local_rows = [
        pltpu.make_async_copy(
            panel.at[lax.rem(c + off, nc), :, columns(l)], shared.at[lax.rem(c + off, nc), l],
            sem_local.at[3 + off])
        for off in range(1, nc)
    ]
    for copy in local_rows:
        copy.start()

    core = cores[l]

    def sketch_pair(p, carry):
        parts = []
        for q in range(2):
            t = 2 * p + q
            block = panel[tiles_ref[1, t]]
            parts.append(dot(probe[t], block, NT))
        pair = dot(jnp.concatenate(parts, axis=0), core, NT, HIGHEST)
        pair = pair.astype(jnp.bfloat16)
        first[l, p] = jnp.concatenate([pair[:rank], pair[rank:]], axis=1)
        return carry

    lax.fori_loop(0, nt // 2, sketch_pair, 0)
    for off in range(1, nl):
        exchange(lambda k: first.at[l], lambda k: first.at[k], s_first, r_first, off).start()

    def pass_shared(off, carry):
        k = next_layer(off)
        for hop in range(1, peers):
            shared_arrival(peer(hop), k).wait_recv()
            if half == 2:
                shared_forward(hop, k).start()
        return carry

    lax.fori_loop(1, nl, pass_shared, 0)
    if half == 2:
        def last_shared(off, carry):
            k = next_layer(off)
            for hop in range(peers):
                shared_arrival(lax.rem(group + hop, peers) * half + (1 - side), k).wait_recv()
            return carry

        lax.fori_loop(1, nl, last_shared, 0)
    for copy in local_rows:
        copy.wait()
    for off in range(1, nl):
        arrival(lambda k: first.at[k], s_first, r_first, next_layer(off)).wait_recv()

    for t in range(nt):
        p, q = t // 2, t % 2
        stack = jnp.concatenate(
            [first[k, p][:, q * rank : (q + 1) * rank] for k in range(nl)], axis=1)
        block = shared[tiles_ref[0, t]].reshape(nl * rank, share)
        rows = dot(stack, block, NN)
        sample[t] = rows
        to, slot = t // per, t % per
        gram_out[to, :, slot * rank : (slot + 1) * rank] = dot(rows, rows, NT, HIGHEST)
    for off in range(1, nl):
        def send_gram(off=off):
            exchange(lambda k: gram_out.at[k], lambda k: gram_in.at[k], s_gram, r_gram, off).start()
        when(all_own, next_layer(off) < owners, send_gram)
    for t in range(nt):
        block = shared[tiles_ref[0, t]].reshape(nl * rank, share)
        rows = sample[t]
        high = rows.astype(jnp.bfloat16)
        low = (rows - high.astype(jnp.float32)).astype(jnp.bfloat16)
        total = dot(high, block, NT) + dot(low, block, NT)
        proj_out[t // per, t % per] = total.astype(jnp.bfloat16)
    for off in range(1, nl):
        def send_proj(off=off):
            exchange(lambda k: proj_out.at[k], lambda k: proj_in.at[k], s_proj, r_proj, off).start()
        when(all_own, next_layer(off) < owners, send_proj)

    def own_tiles():
        gram = gram_out[l]
        for off in range(1, nl):
            k = next_layer(off)
            arrival(lambda k: gram_in.at[k], s_gram, r_gram, k).wait_recv()
            gram = gram + gram_in[k]
        inverse = invert_factor(gram, rank, per)
        inv[l] = inverse
        for off in range(1, nl):
            exchange(lambda k: inv.at[l], lambda k: inv.at[k], s_inv, r_inv, off).start()
        for off in range(1, nl):
            arrival(lambda k: proj_in.at[k], s_proj, r_proj, next_layer(off)).wait_recv()
        for off in range(1, nl):
            core_arrival(next_layer(off)).wait_recv()
        projected = []
        for slot in range(per):
            total = proj_out[l, slot].astype(jnp.float32)
            for off in range(1, nl):
                total = total + proj_in[next_layer(off), slot].astype(jnp.float32)
            projected.append(
                dot(inverse[:, slot * rank : (slot + 1) * rank], total, NN, HIGHEST))
        for k in range(nl):
            piece = jnp.concatenate(
                [x[:, k * rank : (k + 1) * rank] for x in projected], axis=0)
            piece = dot(piece, cores[k], NT, HIGHEST).astype(jnp.bfloat16)
            for slot in range(per):
                second[l, slot, :, k * rank : (k + 1) * rank] = piece[
                    slot * rank : (slot + 1) * rank]
        for off in range(1, nl):
            exchange(lambda k: second.at[l], lambda k: second.at[k], s_second, r_second, off).start()

    when(all_own, l < owners, own_tiles)

    for off in range(1, nl):
        def take_inverse(off=off):
            arrival(lambda k: inv.at[k], s_inv, r_inv, next_layer(off)).wait_recv()
        when(all_own, next_layer(off) < owners, take_inverse)
    scale = math.sqrt(order)
    for t in range(nt):
        slot = t % per
        inverse = inv[t // per][:, slot * rank : (slot + 1) * rank]
        basis_ref[t] = dot(inverse, sample[t], NN, HIGHEST) * scale
    for off in range(1, nl):
        def take_second(off=off):
            arrival(lambda k: second.at[k], s_second, r_second, next_layer(off)).wait_recv()
        when(all_own, next_layer(off) < owners, take_second)
    for t in range(nt):
        block = shared[tiles_ref[1, t]].reshape(nl * rank, share)
        right_ref[t] = dot(second[t // per, t % per], block, NN)

    for off in range(1, nl):
        core_copy(off).wait_send()
        rows_copy(off).wait_send()
        exchange(lambda k: first.at[l], lambda k: first.at[k], s_first, r_first, off).wait_send()

        def sent_sums(off=off):
            exchange(lambda k: gram_out.at[k], lambda k: gram_in.at[k], s_gram, r_gram,
                     off).wait_send()
            exchange(lambda k: proj_out.at[k], lambda k: proj_in.at[k], s_proj, r_proj,
                     off).wait_send()
        when(all_own, next_layer(off) < owners, sent_sums)

        def sent_results(off=off):
            exchange(lambda k: inv.at[l], lambda k: inv.at[k], s_inv, r_inv, off).wait_send()
            exchange(lambda k: second.at[l], lambda k: second.at[k], s_second, r_second,
                     off).wait_send()
        when(all_own, l < owners, sent_results)
        if not all_own:
            def unused_cores(off=off):
                core_arrival(next_layer(off)).wait_recv()
            pl.when(l >= owners)(unused_cores)
    for off in range(1, peers):
        panel_copy(off).wait_send()
    if half == 2:
        for off in range(peers):
            panel_forward(off).wait_send()

    def sent_shared(off, carry):
        k = next_layer(off)
        for hop in range(1, peers):
            shared_copy(hop, k).wait_send()
        if half == 2:
            for hop in range(peers):
                shared_forward(hop, k).wait_send()
        return carry

    lax.fori_loop(1, nl, sent_shared, 0)


def local(nl, nc, factors, cores, tile_list, probes):
    order, nt, rank = probes.shape
    share = order // nl
    per = -(-nt // nl)
    factor = jnp.transpose(factors, (0, 1, 3, 2)).reshape(rank, order)
    probe = jnp.transpose(probes, (1, 2, 0))
    f32, bf16 = jnp.float32, jnp.bfloat16
    dma = pltpu.SemaphoreType.DMA
    out = jax.ShapeDtypeStruct((nt, rank, share), f32)
    basis, right = pl.pallas_call(
        functools.partial(kernel, nl, nc),
        out_shape=(out, out),
        in_specs=[
            pl.BlockSpec(memory_space=pltpu.SMEM),
            pl.BlockSpec(memory_space=pl.ANY),
            pl.BlockSpec(memory_space=pl.ANY),
            pl.BlockSpec(memory_space=pl.ANY),
        ],
        out_specs=[pl.BlockSpec(memory_space=pltpu.VMEM)] * 2,
        scratch_shapes=[
            pltpu.VMEM((nc, rank, order), bf16),
            pltpu.VMEM((nc, nl, rank, share), bf16),
            pltpu.VMEM((nt, rank, order), bf16),
            pltpu.VMEM((nl, rank, rank), f32),
            pltpu.VMEM((nl, nt // 2, rank, 2 * rank), bf16),
            pltpu.VMEM((nt, rank, share), f32),
            pltpu.VMEM((nl, rank, per * rank), f32),
            pltpu.VMEM((nl, rank, per * rank), f32),
            pltpu.VMEM((nl, per, rank, nl * rank), bf16),
            pltpu.VMEM((nl, per, rank, nl * rank), bf16),
            pltpu.VMEM((nl, rank, per * rank), f32),
            pltpu.VMEM((nl, per, rank, nl * rank), bf16),
            dma((3 + nc,)),
            dma((nl,)), dma((nl,)),
            dma((nc,)), dma((nc,)), dma((nc,)),
            dma((nl,)), dma((nl,)),
            dma((nc, nl)), dma((nc, nl)), dma((nc, nl)),
            dma((nl,)), dma((nl,)),
            dma((nl,)), dma((nl,)),
            dma((nl,)), dma((nl,)),
            dma((nl,)), dma((nl,)),
            dma((nl,)), dma((nl,)),
        ],
        compiler_params=pltpu.CompilerParams(
            collective_id=0, has_side_effects=True, vmem_limit_bytes=44 * 1024 * 1024),
    )(jnp.transpose(tile_list), factor, cores.reshape(rank, rank), probe)
    return jnp.transpose(basis, (2, 0, 1)), jnp.transpose(right, (2, 0, 1))


def solution(mesh):
    placed = (
        P("layer", "col", None, None),
        P("layer", None, None),
        P("col", None),
        P(None, "col", None),
    )
    return jax.shard_map(
        functools.partial(local, mesh.shape["layer"], mesh.shape["col"]),
        mesh=mesh,
        in_specs=placed,
        out_specs=(P("layer", "col", None), P("layer", "col", None)),
        check_vma=False,
    )
```

```python
import functools
import math

import jax
import jax.numpy as jnp
from jax import lax
from jax.experimental import pallas as pl
from jax.experimental.pallas import tpu as pltpu
from jax.sharding import PartitionSpec as P

MESH = pl.DeviceIdType.MESH
HIGHEST = lax.Precision.HIGHEST
NN = (((1,), (0,)), ((), ()))
NT = (((1,), (1,)), ((), ()))


def dot(a, b, dims, precision=None):
    return lax.dot_general(a, b, dims, precision=precision, preferred_element_type=jnp.float32)


def invert_factor(gram, rank, count, width=4, depth=8):
    lanes = gram.shape[1]
    row = lax.broadcasted_iota(jnp.int32, gram.shape, 0)
    lane = lax.broadcasted_iota(jnp.int32, gram.shape, 1)
    block = lane // rank
    rest = gram
    inverse = jnp.where(row == lane % rank, 1.0, 0.0).astype(jnp.float32)
    finished = []
    for base in range(0, rank, depth):
        height = rank - base
        shape = (height, lanes)
        index, place = row[:height], block[:height]
        pivots = jnp.ones((depth, lanes), jnp.float32)
        for start in range(0, depth, width):
            columns = []
            for a in range(width):
                at = base + start + a
                column = jnp.broadcast_to(rest[:, at : at + 1], shape)
                for q in range(1, count):
                    at += rank
                    other = jnp.broadcast_to(rest[:, at : at + 1], shape)
                    column = jnp.where(place == q, other, column)
                columns.append(column)
            for a in range(width):
                j = start + a
                pivot = columns[a][j : j + 1, :]
                pivots = jnp.where(index[:depth] == j, pivot, pivots)
                scale = jnp.where(index > j, columns[a] * (1.0 / pivot), 0.0)
                for b in range(a + 1, width):
                    columns[b] = columns[b] - scale * columns[b][j : j + 1, :]
                inverse = inverse - scale * inverse[j : j + 1, :]
                rest = rest - scale * rest[j : j + 1, :]
        root = lax.rsqrt(pivots)
        root = root * (1.5 - 0.5 * pivots * root * root)
        finished.append(inverse[:depth] * root)
        rest, inverse = rest[depth:], inverse[depth:]
    return jnp.concatenate(finished, axis=0)


def split(x):
    high = x.astype(jnp.bfloat16)
    return high, (x - high.astype(jnp.float32)).astype(jnp.bfloat16)


def kernel(nl, nc, tiles_ref, factor_ref, core_ref, probe_ref, basis_ref, right_ref,
           panel, shared, probe, cores, first, sample, gram_out, gram_in, proj_out, proj_in,
           inv, second, sem_local, s_core, r_core, s_panel, r_panel, f_panel, s_rows, r_rows,
           s_shared, f_shared, r_shared, s_first, r_first, s_gram, r_gram, s_proj, r_proj,
           s_inv, r_inv, s_second, r_second):
    l, c = lax.axis_index("layer"), lax.axis_index("col")
    rank, order = factor_ref.shape
    nt = probe_ref.shape[0]
    share = order // nl
    per = -(-nt // nl)
    owners = nt // per
    half = 2 if nc % 2 == 0 else 1
    peers = nc // half
    group, side = c // half, c % half
    other = group * half + (half - 1 - side)

    def at_layer(k):
        return (k, c)

    def at_col(d):
        return (l, d)

    def peer(off):
        return lax.rem(group + off, peers) * half + side

    def next_layer(off):
        return lax.rem(l + off, nl)

    def remote(src, dst, send, recv, device):
        return pltpu.make_async_remote_copy(
            src_ref=src, dst_ref=dst, send_sem=send, recv_sem=recv, device_id=device,
            device_id_type=MESH)

    def when(everyone, pred, body):
        if everyone:
            body()
        else:
            pl.when(pred)(body)

    all_own = owners == nl

    def columns(k):
        return pl.ds(pl.multiple_of(k * share, share), share)

    barrier = pltpu.get_barrier_semaphore()
    for off in range(1, nl):
        pl.semaphore_signal(barrier, inc=1, device_id=at_layer(next_layer(off)), device_id_type=MESH)
    for off in range(1, peers):
        pl.semaphore_signal(barrier, inc=1, device_id=at_col(peer(off)), device_id_type=MESH)
    if half == 2:
        pl.semaphore_signal(barrier, inc=1, device_id=at_col(other), device_id_type=MESH)
    pl.semaphore_wait(barrier, nl - 1 + peers - 1 + half - 1)

    def core_copy(off):
        k = next_layer(off)
        return remote(core_ref, cores.at[l], s_core.at[k], r_core.at[l], at_layer(k))

    def core_arrival(k):
        return remote(core_ref, cores.at[k], s_core.at[k], r_core.at[k], at_layer(k))

    def rows_copy(off):
        k = next_layer(off)
        return remote(factor_ref.at[:, columns(k)], shared.at[c, l], s_rows.at[k], r_rows.at[l],
                      at_layer(k))

    def rows_arrival(k):
        return remote(shared.at[c, k], shared.at[c, k], s_rows.at[k], r_rows.at[k], at_layer(k))

    def panel_copy(off):
        return remote(factor_ref, panel.at[c], s_panel.at[off], r_panel.at[c], at_col(peer(off)))

    def panel_forward(off):
        d = peer(off)
        src = factor_ref if off == 0 else panel.at[d]
        return remote(src, panel.at[d], f_panel.at[off], r_panel.at[d], at_col(other))

    def panel_arrival(d):
        return remote(panel.at[d], panel.at[d], f_panel.at[0], r_panel.at[d], at_col(d))

    def shared_copy(off, k):
        return remote(shared.at[c, k], shared.at[c, k], s_shared.at[off, k], r_shared.at[c, k],
                      at_col(peer(off)))

    def shared_forward(off, k):
        d = peer(off)
        return remote(shared.at[d, k], shared.at[d, k], f_shared.at[off, k], r_shared.at[d, k],
                      at_col(other))

    def shared_arrival(d, k):
        return remote(shared.at[d, k], shared.at[d, k], f_shared.at[0, k], r_shared.at[d, k],
                      at_col(d))

    def exchange(buf_from, buf_to, send, recv, off):
        k = next_layer(off)
        return remote(buf_from(k), buf_to(l), send.at[k], recv.at[l], at_layer(k))

    def arrival(buf_to, send, recv, k):
        return remote(buf_to(k), buf_to(k), send.at[k], recv.at[k], at_layer(k))

    for off in range(1, nl):
        rows_copy(off).start()
    for off in range(1, peers):
        panel_copy(off).start()
    if half == 2:
        panel_forward(0).start()
    for off in range(1, nl):
        core_copy(off).start()
    copies = [
        pltpu.make_async_copy(probe_ref, probe, sem_local.at[0]),
        pltpu.make_async_copy(factor_ref, panel.at[c], sem_local.at[1]),
        pltpu.make_async_copy(factor_ref.at[:, columns(l)], shared.at[c, l], sem_local.at[2]),
        pltpu.make_async_copy(core_ref, cores.at[l], sem_local.at[3]),
    ]
    for copy in copies:
        copy.start()

    for off in range(1, peers):
        panel_arrival(peer(off)).wait_recv()
        if half == 2:
            panel_forward(off).start()

    def send_shared(off, carry):
        k = next_layer(off)
        rows_arrival(k).wait_recv()
        for hop in range(1, peers):
            shared_copy(hop, k).start()
        if half == 2:
            shared_forward(0, k).start()
        return carry

    lax.fori_loop(1, nl, send_shared, 0)
    for copy in copies:
        copy.wait()
    if half == 2:
        for off in range(peers):
            panel_arrival(lax.rem(group + off, peers) * half + (1 - side)).wait_recv()

    local_rows = [
        pltpu.make_async_copy(
            panel.at[lax.rem(c + off, nc), :, columns(l)], shared.at[lax.rem(c + off, nc), l],
            sem_local.at[3 + off])
        for off in range(1, nc)
    ]
    for copy in local_rows:
        copy.start()

    core = cores[l]

    def sketch_pair(p, carry):
        parts = []
        for q in range(2):
            t = 2 * p + q
            block = panel[tiles_ref[1, t]]
            parts.append(dot(probe[t], block, NT))
        pair = dot(jnp.concatenate(parts, axis=0), core, NT, HIGHEST)
        pair = pair.astype(jnp.bfloat16)
        first[l, p] = jnp.concatenate([pair[:rank], pair[rank:]], axis=1)
        return carry

    lax.fori_loop(0, nt // 2, sketch_pair, 0)
    for off in range(1, nl):
        exchange(lambda k: first.at[l], lambda k: first.at[k], s_first, r_first, off).start()

    def pass_shared(off, carry):
        k = next_layer(off)
        for hop in range(1, peers):
            shared_arrival(peer(hop), k).wait_recv()
            if half == 2:
                shared_forward(hop, k).start()
        return carry

    lax.fori_loop(1, nl, pass_shared, 0)
    if half == 2:
        def last_shared(off, carry):
            k = next_layer(off)
            for hop in range(peers):
                shared_arrival(lax.rem(group + hop, peers) * half + (1 - side), k).wait_recv()
            return carry

        lax.fori_loop(1, nl, last_shared, 0)
    for copy in local_rows:
        copy.wait()
    for off in range(1, nl):
        arrival(lambda k: first.at[k], s_first, r_first, next_layer(off)).wait_recv()

    for t in range(nt):
        p, q = t // 2, t % 2
        stack = jnp.concatenate(
            [first[k, p][:, q * rank : (q + 1) * rank] for k in range(nl)], axis=1)
        block = shared[tiles_ref[0, t]].reshape(nl * rank, share)
        high, low = split(dot(stack, block, NN))
        both = jnp.concatenate([high, low], axis=0)
        sample[t] = jnp.concatenate([both, high], axis=0)
        to, slot = t // per, t % per
        product = dot(both, both, NT)
        gram_out[to, :, slot * rank : (slot + 1) * rank] = (
            product[:rank, :rank] + product[rank:, rank:]
            + (product[:rank, rank:] + product[rank:, :rank]))
    for off in range(1, nl):
        def send_gram(off=off):
            exchange(lambda k: gram_out.at[k], lambda k: gram_in.at[k], s_gram, r_gram, off).start()
        when(all_own, next_layer(off) < owners, send_gram)
    for t in range(nt):
        block = shared[tiles_ref[0, t]].reshape(nl * rank, share)
        total = dot(sample[t, : 2 * rank], block, NT)
        total = total[:rank] + total[rank:]
        proj_out[t // per, t % per] = total.astype(jnp.bfloat16)
    for off in range(1, nl):
        def send_proj(off=off):
            exchange(lambda k: proj_out.at[k], lambda k: proj_in.at[k], s_proj, r_proj, off).start()
        when(all_own, next_layer(off) < owners, send_proj)

    def own_tiles():
        gram = gram_out[l]
        for off in range(1, nl):
            k = next_layer(off)
            arrival(lambda k: gram_in.at[k], s_gram, r_gram, k).wait_recv()
            gram = gram + gram_in[k]
        inverse = invert_factor(gram, rank, per)
        inv[l] = inverse
        for off in range(1, nl):
            exchange(lambda k: inv.at[l], lambda k: inv.at[k], s_inv, r_inv, off).start()
        for off in range(1, nl):
            arrival(lambda k: proj_in.at[k], s_proj, r_proj, next_layer(off)).wait_recv()
        for off in range(1, nl):
            core_arrival(next_layer(off)).wait_recv()
        projected = []
        for slot in range(per):
            total = proj_out[l, slot].astype(jnp.float32)
            for off in range(1, nl):
                total = total + proj_in[next_layer(off), slot].astype(jnp.float32)
            projected.append(
                dot(inverse[:, slot * rank : (slot + 1) * rank], total, NN, HIGHEST))
        for k in range(nl):
            piece = jnp.concatenate(
                [x[:, k * rank : (k + 1) * rank] for x in projected], axis=0)
            piece = dot(piece, cores[k], NT, HIGHEST).astype(jnp.bfloat16)
            for slot in range(per):
                second[l, slot, :, k * rank : (k + 1) * rank] = piece[
                    slot * rank : (slot + 1) * rank]
        for off in range(1, nl):
            exchange(lambda k: second.at[l], lambda k: second.at[k], s_second, r_second, off).start()

    when(all_own, l < owners, own_tiles)

    for off in range(1, nl):
        def take_inverse(off=off):
            arrival(lambda k: inv.at[k], s_inv, r_inv, next_layer(off)).wait_recv()
        when(all_own, next_layer(off) < owners, take_inverse)
    scale = math.sqrt(order)
    for t in range(nt):
        slot = t % per
        inverse = inv[t // per][:, slot * rank : (slot + 1) * rank]
        high, low = split(inverse * scale)
        stack = jnp.concatenate([high, high, low], axis=1)
        basis_ref[t] = dot(stack, sample[t], NN)
    for off in range(1, nl):
        def take_second(off=off):
            arrival(lambda k: second.at[k], s_second, r_second, next_layer(off)).wait_recv()
        when(all_own, next_layer(off) < owners, take_second)
    for t in range(nt):
        block = shared[tiles_ref[1, t]].reshape(nl * rank, share)
        right_ref[t] = dot(second[t // per, t % per], block, NN)

    for off in range(1, nl):
        core_copy(off).wait_send()
        rows_copy(off).wait_send()
        exchange(lambda k: first.at[l], lambda k: first.at[k], s_first, r_first, off).wait_send()

        def sent_sums(off=off):
            exchange(lambda k: gram_out.at[k], lambda k: gram_in.at[k], s_gram, r_gram,
                     off).wait_send()
            exchange(lambda k: proj_out.at[k], lambda k: proj_in.at[k], s_proj, r_proj,
                     off).wait_send()
        when(all_own, next_layer(off) < owners, sent_sums)

        def sent_results(off=off):
            exchange(lambda k: inv.at[l], lambda k: inv.at[k], s_inv, r_inv, off).wait_send()
            exchange(lambda k: second.at[l], lambda k: second.at[k], s_second, r_second,
                     off).wait_send()
        when(all_own, l < owners, sent_results)
        if not all_own:
            def unused_cores(off=off):
                core_arrival(next_layer(off)).wait_recv()
            pl.when(l >= owners)(unused_cores)
    for off in range(1, peers):
        panel_copy(off).wait_send()
    if half == 2:
        for off in range(peers):
            panel_forward(off).wait_send()

    def sent_shared(off, carry):
        k = next_layer(off)
        for hop in range(1, peers):
            shared_copy(hop, k).wait_send()
        if half == 2:
            for hop in range(peers):
                shared_forward(hop, k).wait_send()
        return carry

    lax.fori_loop(1, nl, sent_shared, 0)


def local(nl, nc, factors, cores, tile_list, probes):
    order, nt, rank = probes.shape
    share = order // nl
    per = -(-nt // nl)
    factor = jnp.transpose(factors, (0, 1, 3, 2)).reshape(rank, order)
    probe = jnp.transpose(probes, (1, 2, 0))
    f32, bf16 = jnp.float32, jnp.bfloat16
    dma = pltpu.SemaphoreType.DMA
    out = jax.ShapeDtypeStruct((nt, rank, share), f32)
    basis, right = pl.pallas_call(
        functools.partial(kernel, nl, nc),
        out_shape=(out, out),
        in_specs=[
            pl.BlockSpec(memory_space=pltpu.SMEM),
            pl.BlockSpec(memory_space=pltpu.HBM),
            pl.BlockSpec(memory_space=pltpu.HBM),
            pl.BlockSpec(memory_space=pltpu.HBM),
        ],
        out_specs=[pl.BlockSpec(memory_space=pltpu.VMEM)] * 2,
        scratch_shapes=[
            pltpu.VMEM((nc, rank, order), bf16),
            pltpu.VMEM((nc, nl, rank, share), bf16),
            pltpu.VMEM((nt, rank, order), bf16),
            pltpu.VMEM((nl, rank, rank), f32),
            pltpu.VMEM((nl, nt // 2, rank, 2 * rank), bf16),
            pltpu.VMEM((nt, 3 * rank, share), bf16),
            pltpu.VMEM((nl, rank, per * rank), f32),
            pltpu.VMEM((nl, rank, per * rank), f32),
            pltpu.VMEM((nl, per, rank, nl * rank), bf16),
            pltpu.VMEM((nl, per, rank, nl * rank), bf16),
            pltpu.VMEM((nl, rank, per * rank), f32),
            pltpu.VMEM((nl, per, rank, nl * rank), bf16),
            dma((3 + nc,)),
            dma((nl,)), dma((nl,)),
            dma((nc,)), dma((nc,)), dma((nc,)),
            dma((nl,)), dma((nl,)),
            dma((nc, nl)), dma((nc, nl)), dma((nc, nl)),
            dma((nl,)), dma((nl,)),
            dma((nl,)), dma((nl,)),
            dma((nl,)), dma((nl,)),
            dma((nl,)), dma((nl,)),
            dma((nl,)), dma((nl,)),
        ],
        compiler_params=pltpu.CompilerParams(
            collective_id=0, has_side_effects=True, vmem_limit_bytes=60 * 1024 * 1024),
    )(jnp.transpose(tile_list), factor, cores.reshape(rank, rank), probe)
    return jnp.transpose(basis, (2, 0, 1)), jnp.transpose(right, (2, 0, 1))


def solution(mesh):
    placed = (
        P("layer", "col", None, None),
        P("layer", None, None),
        P("col", None),
        P(None, "col", None),
    )
    return jax.shard_map(
        functools.partial(local, mesh.shape["layer"], mesh.shape["col"]),
        mesh=mesh,
        in_specs=placed,
        out_specs=(P("layer", "col", None), P("layer", "col", None)),
        check_vma=False,
    )
```

```python
import functools
import math

import jax
import jax.numpy as jnp
from jax import lax
from jax.experimental import pallas as pl
from jax.experimental.pallas import tpu as pltpu
from jax.sharding import PartitionSpec as P

MESH = pl.DeviceIdType.MESH
HIGHEST = lax.Precision.HIGHEST
NN = (((1,), (0,)), ((), ()))
NT = (((1,), (1,)), ((), ()))


def dot(a, b, dims, precision=None):
    return lax.dot_general(a, b, dims, precision=precision, preferred_element_type=jnp.float32)


def invert_factor(gram, rank, count, midway, width=4, depth=8):
    lanes = gram.shape[1]
    row = lax.broadcasted_iota(jnp.int32, gram.shape, 0)
    lane = lax.broadcasted_iota(jnp.int32, gram.shape, 1)
    block = lane // rank
    rest = gram
    inverse = jnp.where(row == lane % rank, 1.0, 0.0).astype(jnp.float32)
    finished = []
    for base in range(0, rank, depth):
        if base == rank // 2:
            midway()
        height = rank - base
        shape = (height, lanes)
        index, place = row[:height], block[:height]
        pivots = jnp.ones((depth, lanes), jnp.float32)
        for start in range(0, depth, width):
            columns = []
            for a in range(width):
                at = base + start + a
                column = jnp.broadcast_to(rest[:, at : at + 1], shape)
                for q in range(1, count):
                    at += rank
                    other = jnp.broadcast_to(rest[:, at : at + 1], shape)
                    column = jnp.where(place == q, other, column)
                columns.append(column)
            for a in range(width):
                j = start + a
                pivot = columns[a][j : j + 1, :]
                pivots = jnp.where(index[:depth] == j, pivot, pivots)
                scale = jnp.where(index > j, columns[a] * (1.0 / pivot), 0.0)
                for b in range(a + 1, width):
                    columns[b] = columns[b] - scale * columns[b][j : j + 1, :]
                inverse = inverse - scale * inverse[j : j + 1, :]
                rest = rest - scale * rest[j : j + 1, :]
        root = lax.rsqrt(pivots)
        root = root * (1.5 - 0.5 * pivots * root * root)
        finished.append(inverse[:depth] * root)
        rest, inverse = rest[depth:], inverse[depth:]
    return jnp.concatenate(finished, axis=0)


def split(x):
    high = x.astype(jnp.bfloat16)
    return high, (x - high.astype(jnp.float32)).astype(jnp.bfloat16)


def kernel(nl, nc, tiles_ref, factor_ref, core_ref, probe_ref, basis_ref, right_ref,
           panel, shared, probe, cores, first, sample, gram_out, gram_in, proj_out, proj_in,
           inv, second, sem_local, s_core, r_core, s_panel, r_panel, f_panel, s_rows, r_rows,
           s_shared, f_shared, r_shared, s_first, r_first, s_gram, r_gram, s_proj, r_proj,
           s_inv, r_inv, s_second, r_second):
    l, c = lax.axis_index("layer"), lax.axis_index("col")
    rank, order = factor_ref.shape
    nt = probe_ref.shape[0]
    share = order // nl
    per = -(-nt // nl)
    owners = nt // per
    half = 2 if nc % 2 == 0 else 1
    peers = nc // half
    group, side = c // half, c % half
    other = group * half + (half - 1 - side)

    def at_layer(k):
        return (k, c)

    def at_col(d):
        return (l, d)

    def peer(off):
        return lax.rem(group + off, peers) * half + side

    def next_layer(off):
        return lax.rem(l + off, nl)

    def remote(src, dst, send, recv, device):
        return pltpu.make_async_remote_copy(
            src_ref=src, dst_ref=dst, send_sem=send, recv_sem=recv, device_id=device,
            device_id_type=MESH)

    def when(everyone, pred, body):
        if everyone:
            body()
        else:
            pl.when(pred)(body)

    all_own = owners == nl

    def columns(k):
        return pl.ds(pl.multiple_of(k * share, share), share)

    barrier = pltpu.get_barrier_semaphore()
    for off in range(1, nl):
        pl.semaphore_signal(barrier, inc=1, device_id=at_layer(next_layer(off)), device_id_type=MESH)
    for off in range(1, peers):
        pl.semaphore_signal(barrier, inc=1, device_id=at_col(peer(off)), device_id_type=MESH)
    if half == 2:
        pl.semaphore_signal(barrier, inc=1, device_id=at_col(other), device_id_type=MESH)
    pl.semaphore_wait(barrier, nl - 1 + peers - 1 + half - 1)

    def core_copy(off):
        k = next_layer(off)
        return remote(core_ref, cores.at[l], s_core.at[k], r_core.at[l], at_layer(k))

    def core_arrival(k):
        return remote(core_ref, cores.at[k], s_core.at[k], r_core.at[k], at_layer(k))

    def rows_copy(off):
        k = next_layer(off)
        return remote(factor_ref.at[:, columns(k)], shared.at[c, l], s_rows.at[k], r_rows.at[l],
                      at_layer(k))

    def rows_arrival(k):
        return remote(shared.at[c, k], shared.at[c, k], s_rows.at[k], r_rows.at[k], at_layer(k))

    def panel_copy(off):
        return remote(factor_ref, panel.at[c], s_panel.at[off], r_panel.at[c], at_col(peer(off)))

    def panel_forward(off):
        d = peer(off)
        src = factor_ref if off == 0 else panel.at[d]
        return remote(src, panel.at[d], f_panel.at[off], r_panel.at[d], at_col(other))

    def panel_arrival(d):
        return remote(panel.at[d], panel.at[d], f_panel.at[0], r_panel.at[d], at_col(d))

    def shared_copy(off, k):
        return remote(shared.at[c, k], shared.at[c, k], s_shared.at[off, k], r_shared.at[c, k],
                      at_col(peer(off)))

    def shared_forward(off, k):
        d = peer(off)
        return remote(shared.at[d, k], shared.at[d, k], f_shared.at[off, k], r_shared.at[d, k],
                      at_col(other))

    def shared_arrival(d, k):
        return remote(shared.at[d, k], shared.at[d, k], f_shared.at[0, k], r_shared.at[d, k],
                      at_col(d))

    def exchange(buf_from, buf_to, send, recv, off):
        k = next_layer(off)
        return remote(buf_from(k), buf_to(l), send.at[k], recv.at[l], at_layer(k))

    def arrival(buf_to, send, recv, k):
        return remote(buf_to(k), buf_to(k), send.at[k], recv.at[k], at_layer(k))

    for off in range(1, nl):
        rows_copy(off).start()
    for off in range(1, peers):
        panel_copy(off).start()
    if half == 2:
        panel_forward(0).start()
    for off in range(1, nl):
        core_copy(off).start()
    copies = [
        pltpu.make_async_copy(probe_ref, probe, sem_local.at[0]),
        pltpu.make_async_copy(factor_ref, panel.at[c], sem_local.at[1]),
        pltpu.make_async_copy(factor_ref.at[:, columns(l)], shared.at[c, l], sem_local.at[2]),
        pltpu.make_async_copy(core_ref, cores.at[l], sem_local.at[3]),
    ]
    for copy in copies:
        copy.start()

    for off in range(1, peers):
        panel_arrival(peer(off)).wait_recv()
        if half == 2:
            panel_forward(off).start()

    def send_shared(off, carry):
        k = next_layer(off)
        rows_arrival(k).wait_recv()
        for hop in range(1, peers):
            shared_copy(hop, k).start()
        if half == 2:
            shared_forward(0, k).start()
        return carry

    lax.fori_loop(1, nl, send_shared, 0)
    for copy in copies:
        copy.wait()
    if half == 2:
        for off in range(peers):
            panel_arrival(lax.rem(group + off, peers) * half + (1 - side)).wait_recv()

    local_rows = [
        pltpu.make_async_copy(
            panel.at[lax.rem(c + off, nc), :, columns(l)], shared.at[lax.rem(c + off, nc), l],
            sem_local.at[3 + off])
        for off in range(1, nc)
    ]
    for copy in local_rows:
        copy.start()

    core = cores[l]

    def sketch_pair(p, carry):
        parts = []
        for q in range(2):
            t = 2 * p + q
            block = panel[tiles_ref[1, t]]
            parts.append(dot(probe[t], block, NT))
        pair = dot(jnp.concatenate(parts, axis=0), core, NT, HIGHEST)
        pair = pair.astype(jnp.bfloat16)
        first[l, p] = jnp.concatenate([pair[:rank], pair[rank:]], axis=1)
        return carry

    lax.fori_loop(0, nt // 2, sketch_pair, 0)
    for off in range(1, nl):
        exchange(lambda k: first.at[l], lambda k: first.at[k], s_first, r_first, off).start()

    def pass_shared(off, carry):
        k = next_layer(off)
        for hop in range(1, peers):
            shared_arrival(peer(hop), k).wait_recv()
            if half == 2:
                shared_forward(hop, k).start()
        return carry

    lax.fori_loop(1, nl, pass_shared, 0)
    if half == 2:
        def last_shared(off, carry):
            k = next_layer(off)
            for hop in range(peers):
                shared_arrival(lax.rem(group + hop, peers) * half + (1 - side), k).wait_recv()
            return carry

        lax.fori_loop(1, nl, last_shared, 0)
    for copy in local_rows:
        copy.wait()
    for off in range(1, nl):
        arrival(lambda k: first.at[k], s_first, r_first, next_layer(off)).wait_recv()

    for t in range(nt):
        p, q = t // 2, t % 2
        stack = jnp.concatenate(
            [first[k, p][:, q * rank : (q + 1) * rank] for k in range(nl)], axis=1)
        block = shared[tiles_ref[0, t]].reshape(nl * rank, share)
        high, low = split(dot(stack, block, NN))
        both = jnp.concatenate([high, low], axis=0)
        sample[t] = jnp.concatenate([both, high], axis=0)
        to, slot = t // per, t % per
        product = dot(both, both, NT)
        gram_out[to, :, slot * rank : (slot + 1) * rank] = (
            product[:rank, :rank] + product[rank:, rank:]
            + (product[:rank, rank:] + product[rank:, :rank]))
    for off in range(1, nl):
        def send_gram(off=off):
            exchange(lambda k: gram_out.at[k], lambda k: gram_in.at[k], s_gram, r_gram, off).start()
        when(all_own, next_layer(off) < owners, send_gram)
    for t in range(nt):
        block = shared[tiles_ref[0, t]].reshape(nl * rank, share)
        total = dot(sample[t, : 2 * rank], block, NT)
        total = total[:rank] + total[rank:]
        proj_out[t // per, t % per] = total.astype(jnp.bfloat16)
    for off in range(1, nl):
        def send_proj(off=off):
            exchange(lambda k: proj_out.at[k], lambda k: proj_in.at[k], s_proj, r_proj, off).start()
        when(all_own, next_layer(off) < owners, send_proj)

    def own_tiles():
        gram = gram_out[l]
        for off in range(1, nl):
            k = next_layer(off)
            arrival(lambda k: gram_in.at[k], s_gram, r_gram, k).wait_recv()
            gram = gram + gram_in[k]
        inverse = invert_factor(gram, rank, per, send_second)
        inv[l] = inverse
        for off in range(1, nl):
            exchange(lambda k: inv.at[l], lambda k: inv.at[k], s_inv, r_inv, off).start()

    def send_second():
        for off in range(1, nl):
            core_arrival(next_layer(off)).wait_recv()
        for off in range(1, nl):
            arrival(lambda k: proj_in.at[k], s_proj, r_proj, next_layer(off)).wait_recv()
        totals = []
        for slot in range(per):
            total = proj_out[l, slot].astype(jnp.float32)
            for off in range(1, nl):
                total = total + proj_in[next_layer(off), slot].astype(jnp.float32)
            totals.append(total)
        for k in range(nl):
            piece = jnp.concatenate([x[:, k * rank : (k + 1) * rank] for x in totals], axis=0)
            piece = dot(piece, cores[k], NT, HIGHEST).astype(jnp.bfloat16)
            for slot in range(per):
                second[l, slot, :, k * rank : (k + 1) * rank] = piece[
                    slot * rank : (slot + 1) * rank]
        for off in range(1, nl):
            exchange(lambda k: second.at[l], lambda k: second.at[k], s_second, r_second, off).start()

    when(all_own, l < owners, own_tiles)

    scale = math.sqrt(order)
    for off in range(nl):
        def finish(off=off):
            k = next_layer(off)
            if off > 0:
                arrival(lambda k: second.at[k], s_second, r_second, k).wait_recv()
                arrival(lambda k: inv.at[k], s_inv, r_inv, k).wait_recv()
            for slot in range(per):
                t = k * per + slot
                inverse = inv[k][:, slot * rank : (slot + 1) * rank]
                high, low = split(inverse)
                raw = second[k, slot]
                middle = dot(jnp.concatenate([high, low], axis=1),
                             jnp.concatenate([raw, raw], axis=0), NN).astype(jnp.bfloat16)
                block = shared[tiles_ref[1, t]].reshape(nl * rank, share)
                right_ref[t] = dot(middle, block, NN)
                high, low = split(inverse * scale)
                stack = jnp.concatenate([high, high, low], axis=1)
                basis_ref[t] = dot(stack, sample[t], NN)
        when(all_own, next_layer(off) < owners, finish)

    for off in range(1, nl):
        core_copy(off).wait_send()
        rows_copy(off).wait_send()
        exchange(lambda k: first.at[l], lambda k: first.at[k], s_first, r_first, off).wait_send()

        def sent_sums(off=off):
            exchange(lambda k: gram_out.at[k], lambda k: gram_in.at[k], s_gram, r_gram,
                     off).wait_send()
            exchange(lambda k: proj_out.at[k], lambda k: proj_in.at[k], s_proj, r_proj,
                     off).wait_send()
        when(all_own, next_layer(off) < owners, sent_sums)

        def sent_results(off=off):
            exchange(lambda k: inv.at[l], lambda k: inv.at[k], s_inv, r_inv, off).wait_send()
            exchange(lambda k: second.at[l], lambda k: second.at[k], s_second, r_second,
                     off).wait_send()
        when(all_own, l < owners, sent_results)
        if not all_own:
            def unused_cores(off=off):
                core_arrival(next_layer(off)).wait_recv()
            pl.when(l >= owners)(unused_cores)
    for off in range(1, peers):
        panel_copy(off).wait_send()
    if half == 2:
        for off in range(peers):
            panel_forward(off).wait_send()

    def sent_shared(off, carry):
        k = next_layer(off)
        for hop in range(1, peers):
            shared_copy(hop, k).wait_send()
        if half == 2:
            for hop in range(peers):
                shared_forward(hop, k).wait_send()
        return carry

    lax.fori_loop(1, nl, sent_shared, 0)


def local(nl, nc, factors, cores, tile_list, probes):
    order, nt, rank = probes.shape
    share = order // nl
    per = -(-nt // nl)
    factor = jnp.transpose(factors, (0, 1, 3, 2)).reshape(rank, order)
    probe = jnp.transpose(probes, (1, 2, 0))
    f32, bf16 = jnp.float32, jnp.bfloat16
    dma = pltpu.SemaphoreType.DMA
    out = jax.ShapeDtypeStruct((nt, rank, share), f32)
    basis, right = pl.pallas_call(
        functools.partial(kernel, nl, nc),
        out_shape=(out, out),
        in_specs=[
            pl.BlockSpec(memory_space=pltpu.SMEM),
            pl.BlockSpec(memory_space=pltpu.HBM),
            pl.BlockSpec(memory_space=pltpu.HBM),
            pl.BlockSpec(memory_space=pltpu.HBM),
        ],
        out_specs=[pl.BlockSpec(memory_space=pltpu.VMEM)] * 2,
        scratch_shapes=[
            pltpu.VMEM((nc, rank, order), bf16),
            pltpu.VMEM((nc, nl, rank, share), bf16),
            pltpu.VMEM((nt, rank, order), bf16),
            pltpu.VMEM((nl, rank, rank), f32),
            pltpu.VMEM((nl, nt // 2, rank, 2 * rank), bf16),
            pltpu.VMEM((nt, 3 * rank, share), bf16),
            pltpu.VMEM((nl, rank, per * rank), f32),
            pltpu.VMEM((nl, rank, per * rank), f32),
            pltpu.VMEM((nl, per, rank, nl * rank), bf16),
            pltpu.VMEM((nl, per, rank, nl * rank), bf16),
            pltpu.VMEM((nl, rank, per * rank), f32),
            pltpu.VMEM((nl, per, rank, nl * rank), bf16),
            dma((3 + nc,)),
            dma((nl,)), dma((nl,)),
            dma((nc,)), dma((nc,)), dma((nc,)),
            dma((nl,)), dma((nl,)),
            dma((nc, nl)), dma((nc, nl)), dma((nc, nl)),
            dma((nl,)), dma((nl,)),
            dma((nl,)), dma((nl,)),
            dma((nl,)), dma((nl,)),
            dma((nl,)), dma((nl,)),
            dma((nl,)), dma((nl,)),
        ],
        compiler_params=pltpu.CompilerParams(
            collective_id=0, has_side_effects=True, vmem_limit_bytes=60 * 1024 * 1024),
    )(jnp.transpose(tile_list), factor, cores.reshape(rank, rank), probe)
    return jnp.transpose(basis, (2, 0, 1)), jnp.transpose(right, (2, 0, 1))


def solution(mesh):
    placed = (
        P("layer", "col", None, None),
        P("layer", None, None),
        P("col", None),
        P(None, "col", None),
    )
    return jax.shard_map(
        functools.partial(local, mesh.shape["layer"], mesh.shape["col"]),
        mesh=mesh,
        in_specs=placed,
        out_specs=(P("layer", "col", None), P("layer", "col", None)),
        check_vma=False,
    )
```

```python
import functools
import math

import jax
import jax.numpy as jnp
from jax import lax
from jax.experimental import pallas as pl
from jax.experimental.pallas import tpu as pltpu
from jax.sharding import PartitionSpec as P

MESH = pl.DeviceIdType.MESH
HIGHEST = lax.Precision.HIGHEST
NN = (((1,), (0,)), ((), ()))
NT = (((1,), (1,)), ((), ()))


def dot(a, b, dims, precision=None):
    return lax.dot_general(a, b, dims, precision=precision, preferred_element_type=jnp.float32)


def invert_factor(gram, rank, count, width=4, depth=8):
    lanes = gram.shape[1]
    row = lax.broadcasted_iota(jnp.int32, gram.shape, 0)
    lane = lax.broadcasted_iota(jnp.int32, gram.shape, 1)
    block = lane // rank
    rest = gram
    inverse = jnp.where(row == lane % rank, 1.0, 0.0).astype(jnp.float32)
    finished = []
    for base in range(0, rank, depth):
        height = rank - base
        shape = (height, lanes)
        index, place = row[:height], block[:height]
        pivots = jnp.ones((depth, lanes), jnp.float32)
        for start in range(0, depth, width):
            columns = []
            for a in range(width):
                at = base + start + a
                column = jnp.broadcast_to(rest[:, at : at + 1], shape)
                for q in range(1, count):
                    at += rank
                    other = jnp.broadcast_to(rest[:, at : at + 1], shape)
                    column = jnp.where(place == q, other, column)
                columns.append(column)
            for a in range(width):
                j = start + a
                pivot = columns[a][j : j + 1, :]
                pivots = jnp.where(index[:depth] == j, pivot, pivots)
                scale = jnp.where(index > j, columns[a] * (1.0 / pivot), 0.0)
                for b in range(a + 1, width):
                    columns[b] = columns[b] - scale * columns[b][j : j + 1, :]
                inverse = inverse - scale * inverse[j : j + 1, :]
                rest = rest - scale * rest[j : j + 1, :]
        root = lax.rsqrt(pivots)
        root = root * (1.5 - 0.5 * pivots * root * root)
        finished.append(inverse[:depth] * root)
        rest, inverse = rest[depth:], inverse[depth:]
    return jnp.concatenate(finished, axis=0)


def split(x):
    high = x.astype(jnp.bfloat16)
    return high, (x - high.astype(jnp.float32)).astype(jnp.bfloat16)


def kernel(nl, nc, tiles_ref, factor_ref, core_ref, probe_ref, basis_ref, right_ref,
           panel, shared, probe, cores, first, sample, gram_out, gram_in, proj_out, proj_in,
           inv, second, sem_local, s_core, r_core, s_panel, r_panel, f_panel, s_rows, r_rows,
           s_shared, f_shared, r_shared, s_first, r_first, s_gram, r_gram, s_proj, r_proj,
           s_inv, r_inv, s_second, r_second):
    l, c = lax.axis_index("layer"), lax.axis_index("col")
    rank, order = factor_ref.shape
    nt = probe_ref.shape[0]
    share = order // nl
    per = -(-nt // nl)
    owners = nt // per
    half = 2 if nc % 2 == 0 else 1
    peers = nc // half
    group, side = c // half, c % half
    other = group * half + (half - 1 - side)

    def at_layer(k):
        return (k, c)

    def at_col(d):
        return (l, d)

    def peer(off):
        return lax.rem(group + off, peers) * half + side

    def next_layer(off):
        return lax.rem(l + off, nl)

    def remote(src, dst, send, recv, device):
        return pltpu.make_async_remote_copy(
            src_ref=src, dst_ref=dst, send_sem=send, recv_sem=recv, device_id=device,
            device_id_type=MESH)

    def when(everyone, pred, body):
        if everyone:
            body()
        else:
            pl.when(pred)(body)

    all_own = owners == nl

    def columns(k):
        return pl.ds(pl.multiple_of(k * share, share), share)

    barrier = pltpu.get_barrier_semaphore()
    for off in range(1, nl):
        pl.semaphore_signal(barrier, inc=1, device_id=at_layer(next_layer(off)), device_id_type=MESH)
    for off in range(1, peers):
        pl.semaphore_signal(barrier, inc=1, device_id=at_col(peer(off)), device_id_type=MESH)
    if half == 2:
        pl.semaphore_signal(barrier, inc=1, device_id=at_col(other), device_id_type=MESH)
    pl.semaphore_wait(barrier, nl - 1 + peers - 1 + half - 1)

    def core_copy(off):
        k = next_layer(off)
        return remote(core_ref, cores.at[l], s_core.at[k], r_core.at[l], at_layer(k))

    def core_arrival(k):
        return remote(core_ref, cores.at[k], s_core.at[k], r_core.at[k], at_layer(k))

    def rows_copy(off):
        k = next_layer(off)
        return remote(factor_ref.at[:, columns(k)], shared.at[c, l], s_rows.at[k], r_rows.at[l],
                      at_layer(k))

    def rows_arrival(k):
        return remote(shared.at[c, k], shared.at[c, k], s_rows.at[k], r_rows.at[k], at_layer(k))

    def panel_copy(off):
        return remote(factor_ref, panel.at[c], s_panel.at[off], r_panel.at[c], at_col(peer(off)))

    def panel_forward(off):
        d = peer(off)
        src = factor_ref if off == 0 else panel.at[d]
        return remote(src, panel.at[d], f_panel.at[off], r_panel.at[d], at_col(other))

    def panel_arrival(d):
        return remote(panel.at[d], panel.at[d], f_panel.at[0], r_panel.at[d], at_col(d))

    def shared_copy(off, k):
        return remote(shared.at[c, k], shared.at[c, k], s_shared.at[off, k], r_shared.at[c, k],
                      at_col(peer(off)))

    def shared_forward(off, k):
        d = peer(off)
        return remote(shared.at[d, k], shared.at[d, k], f_shared.at[off, k], r_shared.at[d, k],
                      at_col(other))

    def shared_arrival(d, k):
        return remote(shared.at[d, k], shared.at[d, k], f_shared.at[0, k], r_shared.at[d, k],
                      at_col(d))

    def exchange(buf_from, buf_to, send, recv, off):
        k = next_layer(off)
        return remote(buf_from(k), buf_to(l), send.at[k], recv.at[l], at_layer(k))

    def arrival(buf_to, send, recv, k):
        return remote(buf_to(k), buf_to(k), send.at[k], recv.at[k], at_layer(k))

    for off in range(1, nl):
        rows_copy(off).start()
    for off in range(1, peers):
        panel_copy(off).start()
    if half == 2:
        panel_forward(0).start()
    for off in range(1, nl):
        core_copy(off).start()
    copies = [
        pltpu.make_async_copy(probe_ref, probe, sem_local.at[0]),
        pltpu.make_async_copy(factor_ref, panel.at[c], sem_local.at[1]),
        pltpu.make_async_copy(factor_ref.at[:, columns(l)], shared.at[c, l], sem_local.at[2]),
        pltpu.make_async_copy(core_ref, cores.at[l], sem_local.at[3]),
    ]
    for copy in copies:
        copy.start()

    for off in range(1, peers):
        panel_arrival(peer(off)).wait_recv()
        if half == 2:
            panel_forward(off).start()

    def send_shared(off, carry):
        k = next_layer(off)
        rows_arrival(k).wait_recv()
        for hop in range(1, peers):
            shared_copy(hop, k).start()
        if half == 2:
            shared_forward(0, k).start()
        return carry

    lax.fori_loop(1, nl, send_shared, 0)
    for copy in copies:
        copy.wait()
    if half == 2:
        for off in range(peers):
            panel_arrival(lax.rem(group + off, peers) * half + (1 - side)).wait_recv()

    local_rows = [
        pltpu.make_async_copy(
            panel.at[lax.rem(c + off, nc), :, columns(l)], shared.at[lax.rem(c + off, nc), l],
            sem_local.at[3 + off])
        for off in range(1, nc)
    ]
    for copy in local_rows:
        copy.start()

    core = cores[l]

    def sketch_pair(p, carry):
        parts = []
        for q in range(2):
            t = 2 * p + q
            block = panel[tiles_ref[1, t]]
            parts.append(dot(probe[t], block, NT))
        pair = dot(jnp.concatenate(parts, axis=0), core, NT, HIGHEST)
        pair = pair.astype(jnp.bfloat16)
        first[l, p] = jnp.concatenate([pair[:rank], pair[rank:]], axis=1)
        return carry

    lax.fori_loop(0, nt // 2, sketch_pair, 0)
    for off in range(1, nl):
        exchange(lambda k: first.at[l], lambda k: first.at[k], s_first, r_first, off).start()

    def pass_shared(off, carry):
        k = next_layer(off)
        for hop in range(1, peers):
            shared_arrival(peer(hop), k).wait_recv()
            if half == 2:
                shared_forward(hop, k).start()
        return carry

    lax.fori_loop(1, nl, pass_shared, 0)
    if half == 2:
        def last_shared(off, carry):
            k = next_layer(off)
            for hop in range(peers):
                shared_arrival(lax.rem(group + hop, peers) * half + (1 - side), k).wait_recv()
            return carry

        lax.fori_loop(1, nl, last_shared, 0)
    for copy in local_rows:
        copy.wait()
    for off in range(1, nl):
        arrival(lambda k: first.at[k], s_first, r_first, next_layer(off)).wait_recv()

    for t in range(nt):
        p, q = t // 2, t % 2
        stack = jnp.concatenate(
            [first[k, p][:, q * rank : (q + 1) * rank] for k in range(nl)], axis=1)
        block = shared[tiles_ref[0, t]].reshape(nl * rank, share)
        high, low = split(dot(stack, block, NN))
        both = jnp.concatenate([high, low], axis=0)
        sample[t] = jnp.concatenate([both, high], axis=0)
        to, slot = t // per, t % per
        product = dot(both, both, NT)
        gram_out[to, :, slot * rank : (slot + 1) * rank] = (
            product[:rank, :rank] + product[rank:, rank:]
            + (product[:rank, rank:] + product[rank:, :rank]))
        total = dot(both, block, NT)
        proj_out[to, slot] = (total[:rank] + total[rank:]).astype(jnp.bfloat16)
        if slot == per - 1:
            @pl.when(l != to)
            def send_sums(to=to):
                remote(gram_out.at[to], gram_in.at[l], s_gram.at[to], r_gram.at[l],
                       at_layer(to)).start()
                remote(proj_out.at[to], proj_in.at[l], s_proj.at[to], r_proj.at[l],
                       at_layer(to)).start()

    def own_tiles():
        gram = gram_out[l]
        for off in range(1, nl):
            k = next_layer(off)
            arrival(lambda k: gram_in.at[k], s_gram, r_gram, k).wait_recv()
            gram = gram + gram_in[k]
        inverse = invert_factor(gram, rank, per)
        inv[l] = inverse
        for off in range(1, nl):
            exchange(lambda k: inv.at[l], lambda k: inv.at[k], s_inv, r_inv, off).start()
        for off in range(1, nl):
            arrival(lambda k: proj_in.at[k], s_proj, r_proj, next_layer(off)).wait_recv()
        for off in range(1, nl):
            core_arrival(next_layer(off)).wait_recv()
        projected = []
        for slot in range(per):
            total = proj_out[l, slot].astype(jnp.float32)
            for off in range(1, nl):
                total = total + proj_in[next_layer(off), slot].astype(jnp.float32)
            projected.append(
                dot(inverse[:, slot * rank : (slot + 1) * rank], total, NN, HIGHEST))
        for k in range(nl):
            piece = jnp.concatenate(
                [x[:, k * rank : (k + 1) * rank] for x in projected], axis=0)
            piece = dot(piece, cores[k], NT, HIGHEST).astype(jnp.bfloat16)
            for slot in range(per):
                second[l, slot, :, k * rank : (k + 1) * rank] = piece[
                    slot * rank : (slot + 1) * rank]
        for off in range(1, nl):
            exchange(lambda k: second.at[l], lambda k: second.at[k], s_second, r_second, off).start()

    when(all_own, l < owners, own_tiles)

    for off in range(1, nl):
        def take_inverse(off=off):
            arrival(lambda k: inv.at[k], s_inv, r_inv, next_layer(off)).wait_recv()
        when(all_own, next_layer(off) < owners, take_inverse)
    scale = math.sqrt(order)
    for t in range(nt):
        slot = t % per
        inverse = inv[t // per][:, slot * rank : (slot + 1) * rank]
        high, low = split(inverse * scale)
        stack = jnp.concatenate([high, high, low], axis=1)
        basis_ref[t] = dot(stack, sample[t], NN)
    for off in range(1, nl):
        def take_second(off=off):
            arrival(lambda k: second.at[k], s_second, r_second, next_layer(off)).wait_recv()
        when(all_own, next_layer(off) < owners, take_second)
    for t in range(nt):
        block = shared[tiles_ref[1, t]].reshape(nl * rank, share)
        right_ref[t] = dot(second[t // per, t % per], block, NN)

    for off in range(1, nl):
        core_copy(off).wait_send()
        rows_copy(off).wait_send()
        exchange(lambda k: first.at[l], lambda k: first.at[k], s_first, r_first, off).wait_send()

        def sent_sums(off=off):
            exchange(lambda k: gram_out.at[k], lambda k: gram_in.at[k], s_gram, r_gram,
                     off).wait_send()
            exchange(lambda k: proj_out.at[k], lambda k: proj_in.at[k], s_proj, r_proj,
                     off).wait_send()
        when(all_own, next_layer(off) < owners, sent_sums)

        def sent_results(off=off):
            exchange(lambda k: inv.at[l], lambda k: inv.at[k], s_inv, r_inv, off).wait_send()
            exchange(lambda k: second.at[l], lambda k: second.at[k], s_second, r_second,
                     off).wait_send()
        when(all_own, l < owners, sent_results)
        if not all_own:
            def unused_cores(off=off):
                core_arrival(next_layer(off)).wait_recv()
            pl.when(l >= owners)(unused_cores)
    for off in range(1, peers):
        panel_copy(off).wait_send()
    if half == 2:
        for off in range(peers):
            panel_forward(off).wait_send()

    def sent_shared(off, carry):
        k = next_layer(off)
        for hop in range(1, peers):
            shared_copy(hop, k).wait_send()
        if half == 2:
            for hop in range(peers):
                shared_forward(hop, k).wait_send()
        return carry

    lax.fori_loop(1, nl, sent_shared, 0)


def local(nl, nc, factors, cores, tile_list, probes):
    order, nt, rank = probes.shape
    share = order // nl
    per = -(-nt // nl)
    factor = jnp.transpose(factors, (0, 1, 3, 2)).reshape(rank, order)
    probe = jnp.transpose(probes, (1, 2, 0))
    f32, bf16 = jnp.float32, jnp.bfloat16
    dma = pltpu.SemaphoreType.DMA
    out = jax.ShapeDtypeStruct((nt, rank, share), f32)
    basis, right = pl.pallas_call(
        functools.partial(kernel, nl, nc),
        out_shape=(out, out),
        in_specs=[
            pl.BlockSpec(memory_space=pltpu.SMEM),
            pl.BlockSpec(memory_space=pltpu.HBM),
            pl.BlockSpec(memory_space=pltpu.HBM),
            pl.BlockSpec(memory_space=pltpu.HBM),
        ],
        out_specs=[pl.BlockSpec(memory_space=pltpu.VMEM)] * 2,
        scratch_shapes=[
            pltpu.VMEM((nc, rank, order), bf16),
            pltpu.VMEM((nc, nl, rank, share), bf16),
            pltpu.VMEM((nt, rank, order), bf16),
            pltpu.VMEM((nl, rank, rank), f32),
            pltpu.VMEM((nl, nt // 2, rank, 2 * rank), bf16),
            pltpu.VMEM((nt, 3 * rank, share), bf16),
            pltpu.VMEM((nl, rank, per * rank), f32),
            pltpu.VMEM((nl, rank, per * rank), f32),
            pltpu.VMEM((nl, per, rank, nl * rank), bf16),
            pltpu.VMEM((nl, per, rank, nl * rank), bf16),
            pltpu.VMEM((nl, rank, per * rank), f32),
            pltpu.VMEM((nl, per, rank, nl * rank), bf16),
            dma((3 + nc,)),
            dma((nl,)), dma((nl,)),
            dma((nc,)), dma((nc,)), dma((nc,)),
            dma((nl,)), dma((nl,)),
            dma((nc, nl)), dma((nc, nl)), dma((nc, nl)),
            dma((nl,)), dma((nl,)),
            dma((nl,)), dma((nl,)),
            dma((nl,)), dma((nl,)),
            dma((nl,)), dma((nl,)),
            dma((nl,)), dma((nl,)),
        ],
        compiler_params=pltpu.CompilerParams(
            collective_id=0, has_side_effects=True, vmem_limit_bytes=60 * 1024 * 1024),
    )(jnp.transpose(tile_list), factor, cores.reshape(rank, rank), probe)
    return jnp.transpose(basis, (2, 0, 1)), jnp.transpose(right, (2, 0, 1))


def solution(mesh):
    placed = (
        P("layer", "col", None, None),
        P("layer", None, None),
        P("col", None),
        P(None, "col", None),
    )
    return jax.shard_map(
        functools.partial(local, mesh.shape["layer"], mesh.shape["col"]),
        mesh=mesh,
        in_specs=placed,
        out_specs=(P("layer", "col", None), P("layer", "col", None)),
        check_vma=False,
    )
```

```python
import functools
import math

import jax
import jax.numpy as jnp
from jax import lax
from jax.experimental import pallas as pl
from jax.experimental.pallas import tpu as pltpu
from jax.sharding import PartitionSpec as P

MESH = pl.DeviceIdType.MESH
HIGHEST = lax.Precision.HIGHEST
NN = (((1,), (0,)), ((), ()))
NT = (((1,), (1,)), ((), ()))


def dot(a, b, dims, precision=None):
    return lax.dot_general(a, b, dims, precision=precision, preferred_element_type=jnp.float32)


def invert_factor(gram, rank, count, width=4, depth=8):
    lanes = gram.shape[1]
    row = lax.broadcasted_iota(jnp.int32, gram.shape, 0)
    lane = lax.broadcasted_iota(jnp.int32, gram.shape, 1)
    block = lane // rank
    rest = gram
    inverse = jnp.where(row == lane % rank, 1.0, 0.0).astype(jnp.float32)
    finished = []
    for base in range(0, rank, depth):
        height = rank - base
        shape = (height, lanes)
        index, place = row[:height], block[:height]
        pivots = jnp.ones((depth, lanes), jnp.float32)
        for start in range(0, depth, width):
            columns = []
            for a in range(width):
                at = base + start + a
                column = jnp.broadcast_to(rest[:, at : at + 1], shape)
                for q in range(1, count):
                    at += rank
                    other = jnp.broadcast_to(rest[:, at : at + 1], shape)
                    column = jnp.where(place == q, other, column)
                columns.append(column)
            for a in range(width):
                j = start + a
                pivot = columns[a][j : j + 1, :]
                pivots = jnp.where(index[:depth] == j, pivot, pivots)
                scale = jnp.where(index > j, columns[a] * (1.0 / pivot), 0.0)
                for b in range(a + 1, width):
                    columns[b] = columns[b] - scale * columns[b][j : j + 1, :]
                inverse = inverse - scale * inverse[j : j + 1, :]
                rest = rest - scale * rest[j : j + 1, :]
        root = lax.rsqrt(pivots)
        root = root * (1.5 - 0.5 * pivots * root * root)
        finished.append(inverse[:depth] * root)
        rest, inverse = rest[depth:], inverse[depth:]
    return jnp.concatenate(finished, axis=0)


def split(x):
    high = x.astype(jnp.bfloat16)
    return high, (x - high.astype(jnp.float32)).astype(jnp.bfloat16)


def kernel(nl, nc, tiles_ref, factor_ref, core_ref, probe_ref, basis_ref, right_ref,
           panel, shared, probe, cores, first, sample, gram_out, gram_in, proj_out, proj_in,
           inv, second, sem_local, s_core, r_core, s_panel, r_panel, f_panel, s_rows, r_rows,
           s_shared, f_shared, r_shared, s_first, r_first, s_gram, r_gram, s_proj, r_proj,
           s_inv, r_inv, s_second, r_second):
    l, c = lax.axis_index("layer"), lax.axis_index("col")
    rank, order = factor_ref.shape
    nt = probe_ref.shape[0]
    share = order // nl
    per = -(-nt // nl)
    owners = nt // per
    half = 2 if nc % 2 == 0 else 1
    peers = nc // half
    group, side = c // half, c % half
    other = group * half + (half - 1 - side)

    def at_layer(k):
        return (k, c)

    def at_col(d):
        return (l, d)

    def peer(off):
        return lax.rem(group + off, peers) * half + side

    def next_layer(off):
        return lax.rem(l + off, nl)

    def remote(src, dst, send, recv, device):
        return pltpu.make_async_remote_copy(
            src_ref=src, dst_ref=dst, send_sem=send, recv_sem=recv, device_id=device,
            device_id_type=MESH)

    def when(everyone, pred, body):
        if everyone:
            body()
        else:
            pl.when(pred)(body)

    all_own = owners == nl

    def columns(k):
        return pl.ds(pl.multiple_of(k * share, share), share)

    barrier = pltpu.get_barrier_semaphore()
    for off in range(1, nl):
        pl.semaphore_signal(barrier, inc=1, device_id=at_layer(next_layer(off)), device_id_type=MESH)
    for off in range(1, peers):
        pl.semaphore_signal(barrier, inc=1, device_id=at_col(peer(off)), device_id_type=MESH)
    if half == 2:
        pl.semaphore_signal(barrier, inc=1, device_id=at_col(other), device_id_type=MESH)
    pl.semaphore_wait(barrier, nl - 1 + peers - 1 + half - 1)

    def core_copy(off):
        k = next_layer(off)
        return remote(core_ref, cores.at[l], s_core.at[k], r_core.at[l], at_layer(k))

    def core_arrival(k):
        return remote(core_ref, cores.at[k], s_core.at[k], r_core.at[k], at_layer(k))

    def rows_copy(off):
        k = next_layer(off)
        return remote(factor_ref.at[:, columns(k)], shared.at[c, l], s_rows.at[k], r_rows.at[l],
                      at_layer(k))

    def rows_arrival(k):
        return remote(shared.at[c, k], shared.at[c, k], s_rows.at[k], r_rows.at[k], at_layer(k))

    def panel_copy(off):
        return remote(factor_ref, panel.at[c], s_panel.at[off], r_panel.at[c], at_col(peer(off)))

    def panel_forward(off):
        d = peer(off)
        src = factor_ref if off == 0 else panel.at[d]
        return remote(src, panel.at[d], f_panel.at[off], r_panel.at[d], at_col(other))

    def panel_arrival(d):
        return remote(panel.at[d], panel.at[d], f_panel.at[0], r_panel.at[d], at_col(d))

    def shared_copy(off, k):
        return remote(shared.at[c, k], shared.at[c, k], s_shared.at[off, k], r_shared.at[c, k],
                      at_col(peer(off)))

    def shared_forward(off, k):
        d = peer(off)
        return remote(shared.at[d, k], shared.at[d, k], f_shared.at[off, k], r_shared.at[d, k],
                      at_col(other))

    def shared_arrival(d, k):
        return remote(shared.at[d, k], shared.at[d, k], f_shared.at[0, k], r_shared.at[d, k],
                      at_col(d))

    def exchange(buf_from, buf_to, send, recv, off):
        k = next_layer(off)
        return remote(buf_from(k), buf_to(l), send.at[k], recv.at[l], at_layer(k))

    def arrival(buf_to, send, recv, k):
        return remote(buf_to(k), buf_to(k), send.at[k], recv.at[k], at_layer(k))

    for off in range(1, nl):
        rows_copy(off).start()
    for off in range(1, peers):
        panel_copy(off).start()
    if half == 2:
        panel_forward(0).start()
    for off in range(1, nl):
        core_copy(off).start()
    copies = [
        pltpu.make_async_copy(probe_ref, probe, sem_local.at[0]),
        pltpu.make_async_copy(factor_ref, panel.at[c], sem_local.at[1]),
        pltpu.make_async_copy(factor_ref.at[:, columns(l)], shared.at[c, l], sem_local.at[2]),
        pltpu.make_async_copy(core_ref, cores.at[l], sem_local.at[3]),
    ]
    for copy in copies:
        copy.start()

    for off in range(1, peers):
        panel_arrival(peer(off)).wait_recv()
        if half == 2:
            panel_forward(off).start()

    def send_shared(off, carry):
        k = next_layer(off)
        rows_arrival(k).wait_recv()
        for hop in range(1, peers):
            shared_copy(hop, k).start()
        if half == 2:
            shared_forward(0, k).start()
        return carry

    lax.fori_loop(1, nl, send_shared, 0)
    for copy in copies:
        copy.wait()
    if half == 2:
        for off in range(peers):
            panel_arrival(lax.rem(group + off, peers) * half + (1 - side)).wait_recv()

    local_rows = [
        pltpu.make_async_copy(
            panel.at[lax.rem(c + off, nc), :, columns(l)], shared.at[lax.rem(c + off, nc), l],
            sem_local.at[3 + off])
        for off in range(1, nc)
    ]
    for copy in local_rows:
        copy.start()

    core = cores[l]

    def sketch_pair(p, carry):
        parts = []
        for q in range(2):
            t = 2 * p + q
            block = panel[tiles_ref[1, t]]
            parts.append(dot(probe[t], block, NT))
        pair = dot(jnp.concatenate(parts, axis=0), core, NT, HIGHEST)
        pair = pair.astype(jnp.bfloat16)
        first[l, p] = jnp.concatenate([pair[:rank], pair[rank:]], axis=1)
        return carry

    lax.fori_loop(0, nt // 2, sketch_pair, 0)
    for off in range(1, nl):
        exchange(lambda k: first.at[l], lambda k: first.at[k], s_first, r_first, off).start()

    def pass_shared(off, carry):
        k = next_layer(off)
        for hop in range(1, peers):
            shared_arrival(peer(hop), k).wait_recv()
            if half == 2:
                shared_forward(hop, k).start()
        return carry

    lax.fori_loop(1, nl, pass_shared, 0)
    if half == 2:
        def last_shared(off, carry):
            k = next_layer(off)
            for hop in range(peers):
                shared_arrival(lax.rem(group + hop, peers) * half + (1 - side), k).wait_recv()
            return carry

        lax.fori_loop(1, nl, last_shared, 0)
    for copy in local_rows:
        copy.wait()
    for off in range(1, nl):
        arrival(lambda k: first.at[k], s_first, r_first, next_layer(off)).wait_recv()

    for t in range(nt):
        p, q = t // 2, t % 2
        stack = jnp.concatenate(
            [first[k, p][:, q * rank : (q + 1) * rank] for k in range(nl)], axis=1)
        block = shared[tiles_ref[0, t]].reshape(nl * rank, share)
        high, low = split(dot(stack, block, NN))
        both = jnp.concatenate([high, low], axis=0)
        sample[t] = jnp.concatenate([both, high], axis=0)
        to, slot = t // per, t % per
        product = dot(both, both, NT)
        gram_out[to, :, slot * rank : (slot + 1) * rank] = (
            product[:rank, :rank] + product[rank:, rank:]
            + (product[:rank, rank:] + product[rank:, :rank]))
    for off in range(1, nl):
        def send_gram(off=off):
            exchange(lambda k: gram_out.at[k], lambda k: gram_in.at[k], s_gram, r_gram, off).start()
        when(all_own, next_layer(off) < owners, send_gram)
    for t in range(nt):
        block = shared[tiles_ref[0, t]].reshape(nl * rank, share)
        total = dot(sample[t, : 2 * rank], block, NT)
        total = total[:rank] + total[rank:]
        proj_out[t // per, t % per] = total.astype(jnp.bfloat16)
    for off in range(1, nl):
        def send_proj(off=off):
            exchange(lambda k: proj_out.at[k], lambda k: proj_in.at[k], s_proj, r_proj, off).start()
        when(all_own, next_layer(off) < owners, send_proj)

    def own_tiles():
        gram = gram_out[l]
        for off in range(1, nl):
            k = next_layer(off)
            arrival(lambda k: gram_in.at[k], s_gram, r_gram, k).wait_recv()
            gram = gram + gram_in[k]
        inverse = invert_factor(gram, rank, per)
        inv[l] = inverse
        for off in range(1, nl):
            exchange(lambda k: inv.at[l], lambda k: inv.at[k], s_inv, r_inv, off).start()
        for off in range(1, nl):
            arrival(lambda k: proj_in.at[k], s_proj, r_proj, next_layer(off)).wait_recv()
        for off in range(1, nl):
            core_arrival(next_layer(off)).wait_recv()
        projected = []
        for slot in range(per):
            total = proj_out[l, slot].astype(jnp.float32)
            for off in range(1, nl):
                total = total + proj_in[next_layer(off), slot].astype(jnp.float32)
            projected.append(
                dot(inverse[:, slot * rank : (slot + 1) * rank], total, NN, HIGHEST))
        for k in range(nl):
            piece = jnp.concatenate(
                [x[:, k * rank : (k + 1) * rank] for x in projected], axis=0)
            piece = dot(piece, cores[k], NT, HIGHEST).astype(jnp.bfloat16)
            for slot in range(per):
                second[l, slot, :, k * rank : (k + 1) * rank] = piece[
                    slot * rank : (slot + 1) * rank]
        for off in range(1, nl):
            exchange(lambda k: second.at[l], lambda k: second.at[k], s_second, r_second, off).start()

    when(all_own, l < owners, own_tiles)

    scale = math.sqrt(order)
    for off in range(nl):
        def finish_basis(off=off):
            k = next_layer(off)
            if off > 0:
                arrival(lambda k: inv.at[k], s_inv, r_inv, k).wait_recv()
            for slot in range(per):
                t = k * per + slot
                high, low = split(inv[k][:, slot * rank : (slot + 1) * rank] * scale)
                stack = jnp.concatenate([high, high, low], axis=1)
                basis_ref[t] = dot(stack, sample[t], NN)
        when(all_own, next_layer(off) < owners, finish_basis)
    for off in range(nl):
        def finish_right(off=off):
            k = next_layer(off)
            if off > 0:
                arrival(lambda k: second.at[k], s_second, r_second, k).wait_recv()
            for slot in range(per):
                t = k * per + slot
                block = shared[tiles_ref[1, t]].reshape(nl * rank, share)
                right_ref[t] = dot(second[k, slot], block, NN)
        when(all_own, next_layer(off) < owners, finish_right)

    for off in range(1, nl):
        core_copy(off).wait_send()
        rows_copy(off).wait_send()
        exchange(lambda k: first.at[l], lambda k: first.at[k], s_first, r_first, off).wait_send()

        def sent_sums(off=off):
            exchange(lambda k: gram_out.at[k], lambda k: gram_in.at[k], s_gram, r_gram,
                     off).wait_send()
            exchange(lambda k: proj_out.at[k], lambda k: proj_in.at[k], s_proj, r_proj,
                     off).wait_send()
        when(all_own, next_layer(off) < owners, sent_sums)

        def sent_results(off=off):
            exchange(lambda k: inv.at[l], lambda k: inv.at[k], s_inv, r_inv, off).wait_send()
            exchange(lambda k: second.at[l], lambda k: second.at[k], s_second, r_second,
                     off).wait_send()
        when(all_own, l < owners, sent_results)
        if not all_own:
            def unused_cores(off=off):
                core_arrival(next_layer(off)).wait_recv()
            pl.when(l >= owners)(unused_cores)
    for off in range(1, peers):
        panel_copy(off).wait_send()
    if half == 2:
        for off in range(peers):
            panel_forward(off).wait_send()

    def sent_shared(off, carry):
        k = next_layer(off)
        for hop in range(1, peers):
            shared_copy(hop, k).wait_send()
        if half == 2:
            for hop in range(peers):
                shared_forward(hop, k).wait_send()
        return carry

    lax.fori_loop(1, nl, sent_shared, 0)


def local(nl, nc, factors, cores, tile_list, probes):
    order, nt, rank = probes.shape
    share = order // nl
    per = -(-nt // nl)
    factor = jnp.transpose(factors, (0, 1, 3, 2)).reshape(rank, order)
    probe = jnp.transpose(probes, (1, 2, 0))
    f32, bf16 = jnp.float32, jnp.bfloat16
    dma = pltpu.SemaphoreType.DMA
    out = jax.ShapeDtypeStruct((nt, rank, share), f32)
    basis, right = pl.pallas_call(
        functools.partial(kernel, nl, nc),
        out_shape=(out, out),
        in_specs=[
            pl.BlockSpec(memory_space=pltpu.SMEM),
            pl.BlockSpec(memory_space=pltpu.HBM),
            pl.BlockSpec(memory_space=pltpu.HBM),
            pl.BlockSpec(memory_space=pltpu.HBM),
        ],
        out_specs=[pl.BlockSpec(memory_space=pltpu.VMEM)] * 2,
        scratch_shapes=[
            pltpu.VMEM((nc, rank, order), bf16),
            pltpu.VMEM((nc, nl, rank, share), bf16),
            pltpu.VMEM((nt, rank, order), bf16),
            pltpu.VMEM((nl, rank, rank), f32),
            pltpu.VMEM((nl, nt // 2, rank, 2 * rank), bf16),
            pltpu.VMEM((nt, 3 * rank, share), bf16),
            pltpu.VMEM((nl, rank, per * rank), f32),
            pltpu.VMEM((nl, rank, per * rank), f32),
            pltpu.VMEM((nl, per, rank, nl * rank), bf16),
            pltpu.VMEM((nl, per, rank, nl * rank), bf16),
            pltpu.VMEM((nl, rank, per * rank), f32),
            pltpu.VMEM((nl, per, rank, nl * rank), bf16),
            dma((3 + nc,)),
            dma((nl,)), dma((nl,)),
            dma((nc,)), dma((nc,)), dma((nc,)),
            dma((nl,)), dma((nl,)),
            dma((nc, nl)), dma((nc, nl)), dma((nc, nl)),
            dma((nl,)), dma((nl,)),
            dma((nl,)), dma((nl,)),
            dma((nl,)), dma((nl,)),
            dma((nl,)), dma((nl,)),
            dma((nl,)), dma((nl,)),
        ],
        compiler_params=pltpu.CompilerParams(
            collective_id=0, has_side_effects=True, vmem_limit_bytes=60 * 1024 * 1024),
    )(jnp.transpose(tile_list), factor, cores.reshape(rank, rank), probe)
    return jnp.transpose(basis, (2, 0, 1)), jnp.transpose(right, (2, 0, 1))


def solution(mesh):
    placed = (
        P("layer", "col", None, None),
        P("layer", None, None),
        P("col", None),
        P(None, "col", None),
    )
    return jax.shard_map(
        functools.partial(local, mesh.shape["layer"], mesh.shape["col"]),
        mesh=mesh,
        in_specs=placed,
        out_specs=(P("layer", "col", None), P("layer", "col", None)),
        check_vma=False,
    )
```

```python
import functools
import math

import jax
import jax.numpy as jnp
from jax import lax
from jax.experimental import pallas as pl
from jax.experimental.pallas import tpu as pltpu
from jax.sharding import PartitionSpec as P

MESH = pl.DeviceIdType.MESH
HIGHEST = lax.Precision.HIGHEST
NN = (((1,), (0,)), ((), ()))
NT = (((1,), (1,)), ((), ()))


def dot(a, b, dims, precision=None):
    return lax.dot_general(a, b, dims, precision=precision, preferred_element_type=jnp.float32)


def invert_factor(gram, rank, count, width=8, depth=8):
    lanes = gram.shape[1]
    row = lax.broadcasted_iota(jnp.int32, gram.shape, 0)
    lane = lax.broadcasted_iota(jnp.int32, gram.shape, 1)
    block = lane // rank
    rest = gram
    inverse = jnp.where(row == lane % rank, 1.0, 0.0).astype(jnp.float32)
    finished = []
    for base in range(0, rank, depth):
        height = rank - base
        shape = (height, lanes)
        index, place = row[:height], block[:height]
        pivots = jnp.ones((depth, lanes), jnp.float32)
        for start in range(0, depth, width):
            columns = []
            for a in range(width):
                at = base + start + a
                column = jnp.broadcast_to(rest[:, at : at + 1], shape)
                for q in range(1, count):
                    at += rank
                    other = jnp.broadcast_to(rest[:, at : at + 1], shape)
                    column = jnp.where(place == q, other, column)
                columns.append(column)
            for a in range(width):
                j = start + a
                pivot = columns[a][j : j + 1, :]
                pivots = jnp.where(index[:depth] == j, pivot, pivots)
                scale = jnp.where(index > j, columns[a] * (1.0 / pivot), 0.0)
                for b in range(a + 1, width):
                    columns[b] = columns[b] - scale * columns[b][j : j + 1, :]
                inverse = inverse - scale * inverse[j : j + 1, :]
                rest = rest - scale * rest[j : j + 1, :]
        root = lax.rsqrt(pivots)
        root = root * (1.5 - 0.5 * pivots * root * root)
        finished.append(inverse[:depth] * root)
        rest, inverse = rest[depth:], inverse[depth:]
    return jnp.concatenate(finished, axis=0)


def split(x):
    high = x.astype(jnp.bfloat16)
    return high, (x - high.astype(jnp.float32)).astype(jnp.bfloat16)


def kernel(nl, nc, tiles_ref, factor_ref, core_ref, probe_ref, basis_ref, right_ref,
           panel, shared, probe, cores, first, sample, gram_out, gram_in, proj_out, proj_in,
           inv, second, sem_local, s_core, r_core, s_panel, r_panel, f_panel, s_rows, r_rows,
           s_shared, f_shared, r_shared, s_first, r_first, s_gram, r_gram, s_proj, r_proj,
           s_inv, r_inv, s_second, r_second):
    l, c = lax.axis_index("layer"), lax.axis_index("col")
    rank, order = factor_ref.shape
    nt = probe_ref.shape[0]
    share = order // nl
    per = -(-nt // nl)
    owners = nt // per
    half = 2 if nc % 2 == 0 else 1
    peers = nc // half
    group, side = c // half, c % half
    other = group * half + (half - 1 - side)

    def at_layer(k):
        return (k, c)

    def at_col(d):
        return (l, d)

    def peer(off):
        return lax.rem(group + off, peers) * half + side

    def next_layer(off):
        return lax.rem(l + off, nl)

    def remote(src, dst, send, recv, device):
        return pltpu.make_async_remote_copy(
            src_ref=src, dst_ref=dst, send_sem=send, recv_sem=recv, device_id=device,
            device_id_type=MESH)

    def when(everyone, pred, body):
        if everyone:
            body()
        else:
            pl.when(pred)(body)

    all_own = owners == nl

    def columns(k):
        return pl.ds(pl.multiple_of(k * share, share), share)

    barrier = pltpu.get_barrier_semaphore()
    for off in range(1, nl):
        pl.semaphore_signal(barrier, inc=1, device_id=at_layer(next_layer(off)), device_id_type=MESH)
    for off in range(1, peers):
        pl.semaphore_signal(barrier, inc=1, device_id=at_col(peer(off)), device_id_type=MESH)
    if half == 2:
        pl.semaphore_signal(barrier, inc=1, device_id=at_col(other), device_id_type=MESH)
    pl.semaphore_wait(barrier, nl - 1 + peers - 1 + half - 1)

    def core_copy(off):
        k = next_layer(off)
        return remote(core_ref, cores.at[l], s_core.at[k], r_core.at[l], at_layer(k))

    def core_arrival(k):
        return remote(core_ref, cores.at[k], s_core.at[k], r_core.at[k], at_layer(k))

    def rows_copy(off):
        k = next_layer(off)
        return remote(factor_ref.at[:, columns(k)], shared.at[c, l], s_rows.at[k], r_rows.at[l],
                      at_layer(k))

    def rows_arrival(k):
        return remote(shared.at[c, k], shared.at[c, k], s_rows.at[k], r_rows.at[k], at_layer(k))

    def panel_copy(off):
        return remote(factor_ref, panel.at[c], s_panel.at[off], r_panel.at[c], at_col(peer(off)))

    def panel_forward(off):
        d = peer(off)
        src = factor_ref if off == 0 else panel.at[d]
        return remote(src, panel.at[d], f_panel.at[off], r_panel.at[d], at_col(other))

    def panel_arrival(d):
        return remote(panel.at[d], panel.at[d], f_panel.at[0], r_panel.at[d], at_col(d))

    def shared_copy(off, k):
        return remote(shared.at[c, k], shared.at[c, k], s_shared.at[off, k], r_shared.at[c, k],
                      at_col(peer(off)))

    def shared_forward(off, k):
        d = peer(off)
        return remote(shared.at[d, k], shared.at[d, k], f_shared.at[off, k], r_shared.at[d, k],
                      at_col(other))

    def shared_arrival(d, k):
        return remote(shared.at[d, k], shared.at[d, k], f_shared.at[0, k], r_shared.at[d, k],
                      at_col(d))

    def exchange(buf_from, buf_to, send, recv, off):
        k = next_layer(off)
        return remote(buf_from(k), buf_to(l), send.at[k], recv.at[l], at_layer(k))

    def arrival(buf_to, send, recv, k):
        return remote(buf_to(k), buf_to(k), send.at[k], recv.at[k], at_layer(k))

    for off in range(1, nl):
        rows_copy(off).start()
    for off in range(1, peers):
        panel_copy(off).start()
    if half == 2:
        panel_forward(0).start()
    for off in range(1, nl):
        core_copy(off).start()
    copies = [
        pltpu.make_async_copy(probe_ref, probe, sem_local.at[0]),
        pltpu.make_async_copy(factor_ref, panel.at[c], sem_local.at[1]),
        pltpu.make_async_copy(factor_ref.at[:, columns(l)], shared.at[c, l], sem_local.at[2]),
        pltpu.make_async_copy(core_ref, cores.at[l], sem_local.at[3]),
    ]
    for copy in copies:
        copy.start()

    for off in range(1, peers):
        panel_arrival(peer(off)).wait_recv()
        if half == 2:
            panel_forward(off).start()

    def send_shared(off, carry):
        k = next_layer(off)
        rows_arrival(k).wait_recv()
        for hop in range(1, peers):
            shared_copy(hop, k).start()
        if half == 2:
            shared_forward(0, k).start()
        return carry

    lax.fori_loop(1, nl, send_shared, 0)
    for copy in copies:
        copy.wait()
    if half == 2:
        for off in range(peers):
            panel_arrival(lax.rem(group + off, peers) * half + (1 - side)).wait_recv()

    local_rows = [
        pltpu.make_async_copy(
            panel.at[lax.rem(c + off, nc), :, columns(l)], shared.at[lax.rem(c + off, nc), l],
            sem_local.at[3 + off])
        for off in range(1, nc)
    ]
    for copy in local_rows:
        copy.start()

    core = cores[l]

    def sketch_pair(p, carry):
        parts = []
        for q in range(2):
            t = 2 * p + q
            block = panel[tiles_ref[1, t]]
            parts.append(dot(probe[t], block, NT))
        pair = dot(jnp.concatenate(parts, axis=0), core, NT, HIGHEST)
        pair = pair.astype(jnp.bfloat16)
        first[l, p] = jnp.concatenate([pair[:rank], pair[rank:]], axis=1)
        return carry

    lax.fori_loop(0, nt // 2, sketch_pair, 0)
    for off in range(1, nl):
        exchange(lambda k: first.at[l], lambda k: first.at[k], s_first, r_first, off).start()

    def pass_shared(off, carry):
        k = next_layer(off)
        for hop in range(1, peers):
            shared_arrival(peer(hop), k).wait_recv()
            if half == 2:
                shared_forward(hop, k).start()
        return carry

    lax.fori_loop(1, nl, pass_shared, 0)
    if half == 2:
        def last_shared(off, carry):
            k = next_layer(off)
            for hop in range(peers):
                shared_arrival(lax.rem(group + hop, peers) * half + (1 - side), k).wait_recv()
            return carry

        lax.fori_loop(1, nl, last_shared, 0)
    for copy in local_rows:
        copy.wait()
    for off in range(1, nl):
        arrival(lambda k: first.at[k], s_first, r_first, next_layer(off)).wait_recv()

    for t in range(nt):
        p, q = t // 2, t % 2
        stack = jnp.concatenate(
            [first[k, p][:, q * rank : (q + 1) * rank] for k in range(nl)], axis=1)
        block = shared[tiles_ref[0, t]].reshape(nl * rank, share)
        high, low = split(dot(stack, block, NN))
        both = jnp.concatenate([high, low], axis=0)
        sample[t] = jnp.concatenate([both, high], axis=0)
        to, slot = t // per, t % per
        product = dot(both, both, NT)
        gram_out[to, :, slot * rank : (slot + 1) * rank] = (
            product[:rank, :rank] + product[rank:, rank:]
            + (product[:rank, rank:] + product[rank:, :rank]))
    for off in range(1, nl):
        def send_gram(off=off):
            exchange(lambda k: gram_out.at[k], lambda k: gram_in.at[k], s_gram, r_gram, off).start()
        when(all_own, next_layer(off) < owners, send_gram)
    for t in range(nt):
        block = shared[tiles_ref[0, t]].reshape(nl * rank, share)
        total = dot(sample[t, : 2 * rank], block, NT)
        total = total[:rank] + total[rank:]
        proj_out[t // per, t % per] = total.astype(jnp.bfloat16)
    for off in range(1, nl):
        def send_proj(off=off):
            exchange(lambda k: proj_out.at[k], lambda k: proj_in.at[k], s_proj, r_proj, off).start()
        when(all_own, next_layer(off) < owners, send_proj)

    def own_tiles():
        gram = gram_out[l]
        for off in range(1, nl):
            k = next_layer(off)
            arrival(lambda k: gram_in.at[k], s_gram, r_gram, k).wait_recv()
            gram = gram + gram_in[k]
        inverse = invert_factor(gram, rank, per)
        inv[l] = inverse
        for off in range(1, nl):
            exchange(lambda k: inv.at[l], lambda k: inv.at[k], s_inv, r_inv, off).start()
        for off in range(1, nl):
            arrival(lambda k: proj_in.at[k], s_proj, r_proj, next_layer(off)).wait_recv()
        for off in range(1, nl):
            core_arrival(next_layer(off)).wait_recv()
        projected = []
        for slot in range(per):
            total = proj_out[l, slot].astype(jnp.float32)
            for off in range(1, nl):
                total = total + proj_in[next_layer(off), slot].astype(jnp.float32)
            projected.append(
                dot(inverse[:, slot * rank : (slot + 1) * rank], total, NN, HIGHEST))
        for k in range(nl):
            piece = jnp.concatenate(
                [x[:, k * rank : (k + 1) * rank] for x in projected], axis=0)
            piece = dot(piece, cores[k], NT, HIGHEST).astype(jnp.bfloat16)
            for slot in range(per):
                second[l, slot, :, k * rank : (k + 1) * rank] = piece[
                    slot * rank : (slot + 1) * rank]
        for off in range(1, nl):
            exchange(lambda k: second.at[l], lambda k: second.at[k], s_second, r_second, off).start()

    when(all_own, l < owners, own_tiles)

    for off in range(1, nl):
        def take_inverse(off=off):
            arrival(lambda k: inv.at[k], s_inv, r_inv, next_layer(off)).wait_recv()
        when(all_own, next_layer(off) < owners, take_inverse)
    scale = math.sqrt(order)
    for t in range(nt):
        slot = t % per
        inverse = inv[t // per][:, slot * rank : (slot + 1) * rank]
        high, low = split(inverse * scale)
        stack = jnp.concatenate([high, high, low], axis=1)
        basis_ref[t] = dot(stack, sample[t], NN)
    for off in range(1, nl):
        def take_second(off=off):
            arrival(lambda k: second.at[k], s_second, r_second, next_layer(off)).wait_recv()
        when(all_own, next_layer(off) < owners, take_second)
    for t in range(nt):
        block = shared[tiles_ref[1, t]].reshape(nl * rank, share)
        right_ref[t] = dot(second[t // per, t % per], block, NN)

    for off in range(1, nl):
        core_copy(off).wait_send()
        rows_copy(off).wait_send()
        exchange(lambda k: first.at[l], lambda k: first.at[k], s_first, r_first, off).wait_send()

        def sent_sums(off=off):
            exchange(lambda k: gram_out.at[k], lambda k: gram_in.at[k], s_gram, r_gram,
                     off).wait_send()
            exchange(lambda k: proj_out.at[k], lambda k: proj_in.at[k], s_proj, r_proj,
                     off).wait_send()
        when(all_own, next_layer(off) < owners, sent_sums)

        def sent_results(off=off):
            exchange(lambda k: inv.at[l], lambda k: inv.at[k], s_inv, r_inv, off).wait_send()
            exchange(lambda k: second.at[l], lambda k: second.at[k], s_second, r_second,
                     off).wait_send()
        when(all_own, l < owners, sent_results)
        if not all_own:
            def unused_cores(off=off):
                core_arrival(next_layer(off)).wait_recv()
            pl.when(l >= owners)(unused_cores)
    for off in range(1, peers):
        panel_copy(off).wait_send()
    if half == 2:
        for off in range(peers):
            panel_forward(off).wait_send()

    def sent_shared(off, carry):
        k = next_layer(off)
        for hop in range(1, peers):
            shared_copy(hop, k).wait_send()
        if half == 2:
            for hop in range(peers):
                shared_forward(hop, k).wait_send()
        return carry

    lax.fori_loop(1, nl, sent_shared, 0)


def local(nl, nc, factors, cores, tile_list, probes):
    order, nt, rank = probes.shape
    share = order // nl
    per = -(-nt // nl)
    factor = jnp.transpose(factors, (0, 1, 3, 2)).reshape(rank, order)
    probe = jnp.transpose(probes, (1, 2, 0))
    f32, bf16 = jnp.float32, jnp.bfloat16
    dma = pltpu.SemaphoreType.DMA
    out = jax.ShapeDtypeStruct((nt, rank, share), f32)
    basis, right = pl.pallas_call(
        functools.partial(kernel, nl, nc),
        out_shape=(out, out),
        in_specs=[
            pl.BlockSpec(memory_space=pltpu.SMEM),
            pl.BlockSpec(memory_space=pltpu.HBM),
            pl.BlockSpec(memory_space=pltpu.HBM),
            pl.BlockSpec(memory_space=pltpu.HBM),
        ],
        out_specs=[pl.BlockSpec(memory_space=pltpu.VMEM)] * 2,
        scratch_shapes=[
            pltpu.VMEM((nc, rank, order), bf16),
            pltpu.VMEM((nc, nl, rank, share), bf16),
            pltpu.VMEM((nt, rank, order), bf16),
            pltpu.VMEM((nl, rank, rank), f32),
            pltpu.VMEM((nl, nt // 2, rank, 2 * rank), bf16),
            pltpu.VMEM((nt, 3 * rank, share), bf16),
            pltpu.VMEM((nl, rank, per * rank), f32),
            pltpu.VMEM((nl, rank, per * rank), f32),
            pltpu.VMEM((nl, per, rank, nl * rank), bf16),
            pltpu.VMEM((nl, per, rank, nl * rank), bf16),
            pltpu.VMEM((nl, rank, per * rank), f32),
            pltpu.VMEM((nl, per, rank, nl * rank), bf16),
            dma((3 + nc,)),
            dma((nl,)), dma((nl,)),
            dma((nc,)), dma((nc,)), dma((nc,)),
            dma((nl,)), dma((nl,)),
            dma((nc, nl)), dma((nc, nl)), dma((nc, nl)),
            dma((nl,)), dma((nl,)),
            dma((nl,)), dma((nl,)),
            dma((nl,)), dma((nl,)),
            dma((nl,)), dma((nl,)),
            dma((nl,)), dma((nl,)),
        ],
        compiler_params=pltpu.CompilerParams(
            collective_id=0, has_side_effects=True, vmem_limit_bytes=60 * 1024 * 1024),
    )(jnp.transpose(tile_list), factor, cores.reshape(rank, rank), probe)
    return jnp.transpose(basis, (2, 0, 1)), jnp.transpose(right, (2, 0, 1))


def solution(mesh):
    placed = (
        P("layer", "col", None, None),
        P("layer", None, None),
        P("col", None),
        P(None, "col", None),
    )
    return jax.shard_map(
        functools.partial(local, mesh.shape["layer"], mesh.shape["col"]),
        mesh=mesh,
        in_specs=placed,
        out_specs=(P("layer", "col", None), P("layer", "col", None)),
        check_vma=False,
    )
```
